32 devices in a mesh: blk: 4 (over y, x), seg: 8 (over z, core).
Axes of the slice: x: 2, y: 2, z: 4, core: 2. Of those that a mesh axis runs over, the one named last changes fastest.
Arguments:
- spectra: bfloat16 [8, 512, 2, 4096], P(None, ('blk', 'seg')), may hold values from -6 to 6
- fibre_lists: int32 [8, 64], replicated, may hold values from 0 to 511, as said below
- pairing: int32 [1, 8], replicated, may hold values from 0 to 7, as said below
Outputs:
- stack: float32 [1, 8, 64, 64, 128], P(None, 'blk', 'seg')
The draws below stay inside these ranges and needn't reach their ends.
Inputs may be any that keep to these rules, and one draw needn't show every extreme that they name: `fibre_lists`: row b lists the 64 channels of block b in an arbitrary order; every channel number appears exactly once in the table. Within every aligned range of 128 consecutive channel numbers, no block has more than 24 of its channels, and some block has exactly 24. `pairing`: row r maps every block to its partner in round r: the partner of the partner is the block itself, no block is its own partner, and no two rounds pair the same two blocks.
All inputs are finite; a program needn't handle non-finite values.
Results may differ from the reference program's by a relative error of at most 0.0037.
Values may be sent and summed in bfloat16 or wider, within the bound.
A program may use at most 192 MiB of HBM per device.

```python
import math
import jax
import jax.numpy as jnp
from jax import lax

F = 4096
LH = 128
CH = 64
BLK_DEV = 2
ROUNDS = 1
NBLOCKS = 8
SEGMENTS = 8
CHANNELS = 512
MOST = 24


def fibre_helper(key):
    columns = NBLOCKS // BLK_DEV
    width = BLK_DEV * CH
    keys = jax.random.split(key, 5)
    sigma = jax.random.permutation(keys[0], columns)
    shifts = jax.random.permutation(keys[1], NBLOCKS) % columns
    base = (CH - MOST) // (columns - 1)
    extra = (CH - MOST) % (columns - 1)
    weights = jnp.array([MOST] + [base + (1 if position < extra else 0) for position in range(columns - 1)], jnp.int32)
    for position in range(1, columns - 1, 2):
        limit = jnp.minimum(weights[position], MOST - weights[position + 1])
        moved = jax.random.randint(jax.random.fold_in(keys[2], position), (), 0, limit + 1)
        weights = weights.at[position].add(-moved).at[position + 1].add(moved)
    counts = weights[(sigma[:, None] - shifts[None, :]) % columns]
    ends = jnp.cumsum(counts, axis=1)
    places = jnp.arange(width, dtype=jnp.int32)
    block_at = jnp.sum((places[None, :, None] >= ends[:, None, :]).astype(jnp.int32), axis=2)
    orders = jax.vmap(lambda sub_key: jax.random.permutation(sub_key, width))(jax.random.split(keys[3], columns))
    block_of = jnp.zeros((columns, width), jnp.int32).at[jnp.arange(columns)[:, None], orders].set(block_at)
    flat_blocks = block_of.reshape(-1)
    numbers = jnp.arange(columns * width, dtype=jnp.int32)
    sort_keys = jnp.where(flat_blocks[None, :] == jnp.arange(NBLOCKS, dtype=jnp.int32)[:, None], numbers[None, :], columns * width)
    lists = jnp.sort(sort_keys, axis=1)[:, :CH]
    shuffles = jax.vmap(lambda sub_key: jax.random.permutation(sub_key, CH))(jax.random.split(keys[4], NBLOCKS))
    return jnp.take_along_axis(lists, shuffles, axis=1).astype(jnp.int32)


def draw_fibre_lists(key, part):
    return fibre_helper(jax.random.fold_in(key, 11))


def draw_pairing(key, part):
    circle = NBLOCKS - 1
    keys = jax.random.split(jax.random.fold_in(key, 23), 2)
    labels = jax.random.permutation(keys[0], NBLOCKS).astype(jnp.int32)
    chosen = jax.random.permutation(keys[1], circle)[:ROUNDS].astype(jnp.int32)
    blocks = jnp.arange(NBLOCKS, dtype=jnp.int32)

    def one_round(round_id):
        partner = jnp.where(blocks == circle, round_id, jnp.where(blocks == round_id, circle, (2 * round_id - blocks) % circle))
        return jnp.zeros((NBLOCKS,), jnp.int32).at[labels].set(labels[partner])
    return jax.vmap(one_round)(chosen).astype(jnp.int32)


def levels(own_key, extent, pieces, smallest, largest):
    def one(dim, parts):
        steps = jax.random.uniform(jax.random.fold_in(jax.random.fold_in(own_key, 6), dim), (parts,), jnp.float32, smallest / len(pieces), largest / len(pieces))
        return jnp.repeat(jnp.exp(steps), extent[dim] // parts).reshape((-1,) + (1,) * (len(extent) - dim - 1))

    factor_of = one(*pieces[0])
    for cut in pieces[1:]:
        factor_of = factor_of * one(*cut)
    return factor_of


def gaussian(key, dims, scale, reach, cuts=(), held_as=jnp.bfloat16):
    level = levels(key, dims, cuts, -0.22, 0.18) if cuts else 1.0
    result = jax.random.normal(key, dims, jnp.float32) * scale * level
    return jnp.minimum(jnp.maximum(result, -reach), reach).astype(held_as)


def setup_inputs(seed: int = 0) -> dict:
    key_list = jax.random.split(jax.random.key(seed), 4)
    spectra = gaussian(key_list[0], (SEGMENTS, CHANNELS, 2, F), 1.0, 6.0, ((1, 32),))
    fibre_lists = draw_fibre_lists(jax.random.fold_in(key_list[3], 71), 0)
    pairing = draw_pairing(jax.random.fold_in(key_list[3], 71), 0)
    return dict(spectra=spectra, fibre_lists=fibre_lists, pairing=pairing)


def make_table(frequencies, lag_count):
    freq_ids = jnp.arange(frequencies, dtype=jnp.int32)[:, None]
    lag_ids = jnp.arange(lag_count, dtype=jnp.int32)[None, :]
    angles = (freq_ids * lag_ids % (2 * frequencies)).astype(jnp.float32) * (math.pi / frequencies)
    return jnp.concatenate([jnp.cos(angles), -jnp.sin(angles)], 0).astype(jnp.bfloat16)

def cross_lags(left_rows, right_rows, lag_table):
    left_re = left_rows[:, 0].astype(jnp.float32)
    left_im = left_rows[:, 1].astype(jnp.float32)
    right_re = right_rows[:, 0].astype(jnp.float32)
    right_im = right_rows[:, 1].astype(jnp.float32)
    real_part = left_re[:, None, :] * right_re[None] + left_im[:, None, :] * right_im[None]
    imag_part = left_im[:, None, :] * right_re[None] - left_re[:, None, :] * right_im[None]
    spectrum = jnp.concatenate([real_part, imag_part], -1).astype(jnp.bfloat16)
    spectrum = spectrum.reshape(-1, spectrum.shape[-1])
    product = jnp.dot(spectrum, lag_table, preferred_element_type=jnp.float32)
    return product.reshape(left_rows.shape[0], right_rows.shape[0], -1)

def reference(spectra, fibre_lists, pairing):
    lag_table = make_table(F, LH)
    panels = jnp.take(spectra, fibre_lists.reshape(-1), axis=1).reshape(SEGMENTS, NBLOCKS, CH, 2, F)

    def unit_term(unit_index):
        round_id = unit_index // NBLOCKS
        block_id = unit_index % NBLOCKS
        partner = pairing[round_id, block_id]
        own_panel = lax.dynamic_index_in_dim(panels, block_id, 1, keepdims=False)
        other_panel = lax.dynamic_index_in_dim(panels, partner, 1, keepdims=False)

        def accumulate(step, running):
            left_rows = lax.dynamic_index_in_dim(own_panel, step, 0, keepdims=False)
            right_rows = lax.dynamic_index_in_dim(other_panel, step, 0, keepdims=False)
            return running + cross_lags(left_rows, right_rows, lag_table)
        return lax.fori_loop(0, SEGMENTS, accumulate, jnp.zeros((CH, CH, LH), jnp.float32))
    stacks = lax.map(unit_term, jnp.arange(ROUNDS * NBLOCKS, dtype=jnp.int32))
    return stacks.reshape(ROUNDS, NBLOCKS, CH, CH, LH) * (1.0 / math.sqrt(F * SEGMENTS))
```

```python
import functools
import math

import numpy as np
import jax
import jax.numpy as jnp
from jax import lax
from jax.experimental import pallas as pl
from jax.experimental.pallas import tpu as pltpu
from jax.sharding import PartitionSpec as P

LH = 128
STEP = 16
COARSE = LH // STEP
FINE = STEP // 2
CHUNK = 512
NT = (((1,), (1,)), ((), ()))


def phase_tables(frequencies):
    freq = np.arange(frequencies, dtype=np.float64)[None, :]
    coarse = (STEP * np.arange(COARSE, dtype=np.float64) + (STEP - 1) / 2)[:, None]
    fine = (np.arange(FINE, dtype=np.float64) + 0.5)[:, None]
    angles = np.concatenate([coarse, fine], 0) * freq * (math.pi / frequencies)
    return np.cos(angles).astype(np.float32), np.sin(angles).astype(np.float32)


def take_small(table, index):
    hit = index[:, None] == jnp.arange(table.shape[0], dtype=jnp.int32)[None, :]
    return jnp.sum(jnp.where(hit, table[None, :], 0), axis=1)


def assign(partner):
    count = partner.shape[0]
    blocks = jnp.arange(count, dtype=jnp.int32)
    hop = partner ^ 1
    lowest = blocks
    for _ in range(max(1, (count // 2 - 1).bit_length())):
        lowest = jnp.minimum(lowest, take_small(lowest, hop))
        hop = take_small(hop, hop)
    return lowest < take_small(lowest, blocks ^ 1)


def correlate_kernel(chan, arrived, unpack, cos_ref, sin_ref, plus_ref, minus_ref, xp, xm, yp):
    step = pl.program_id(0)
    width = arrived.shape[1]

    @pl.when(step == 0)
    def _():
        plus_ref[...] = jnp.zeros_like(plus_ref)
        minus_ref[...] = jnp.zeros_like(minus_ref)

    rows = jnp.dot(unpack[...], arrived[...], preferred_element_type=jnp.float32)
    xr, yr = rows[0:chan], rows[chan : 2 * chan]
    xi, yi = rows[2 * chan : 3 * chan], rows[3 * chan : 4 * chan]
    re, im = pl.ds(0, width), pl.ds(width, width)
    bf = jnp.bfloat16
    for a in range(COARSE):
        c, s = cos_ref[a : a + 1, :], sin_ref[a : a + 1, :]
        rc, rs, ic, i_s = xr * c, xr * s, xi * c, xi * s
        at = pl.ds(a * chan, chan)
        xp[at, re] = (rc - i_s).astype(bf)
        xp[at, im] = (ic + rs).astype(bf)
        xm[at, re] = (rc + i_s).astype(bf)
        xm[at, im] = (ic - rs).astype(bf)
    for m in range(FINE):
        c, s = cos_ref[COARSE + m : COARSE + m + 1, :], sin_ref[COARSE + m : COARSE + m + 1, :]
        rc, rs, ic, i_s = yr * c, yr * s, yi * c, yi * s
        at, back = pl.ds((FINE + m) * chan, chan), pl.ds((FINE - 1 - m) * chan, chan)
        yp[at, re] = (rc + i_s).astype(bf)
        yp[at, im] = (ic - rs).astype(bf)
        yp[back, re] = (rc - i_s).astype(bf)
        yp[back, im] = (ic + rs).astype(bf)

    tile = 256

    @pl.loop(0, yp.shape[0] // tile)
    def _(t):
        at = pl.ds(pl.multiple_of(t * tile, tile), tile)
        y = yp[at, :]
        plus_ref[:, at] += lax.dot_general(xp[...], y, NT, preferred_element_type=jnp.float32)
        minus_ref[at, :] += lax.dot_general(y, xm[...], NT, preferred_element_type=jnp.float32)


def correlate(arrived, unpack, chan):
    total, frequencies = arrived.shape
    cos, sin = phase_tables(frequencies)
    wide = COARSE * chan
    return pl.pallas_call(
        functools.partial(correlate_kernel, chan),
        grid=(frequencies // CHUNK,),
        in_specs=[
            pl.BlockSpec((total, CHUNK), lambda k: (0, k)),
            pl.BlockSpec(unpack.shape, lambda k: (0, 0)),
            pl.BlockSpec((COARSE + FINE, CHUNK), lambda k: (0, k)),
            pl.BlockSpec((COARSE + FINE, CHUNK), lambda k: (0, k)),
        ],
        out_specs=[
            pl.BlockSpec((wide, 2 * wide), lambda k: (0, 0)),
            pl.BlockSpec((2 * wide, wide), lambda k: (0, 0)),
        ],
        out_shape=[
            jax.ShapeDtypeStruct((wide, 2 * wide), jnp.float32),
            jax.ShapeDtypeStruct((2 * wide, wide), jnp.float32),
        ],
        scratch_shapes=[
            pltpu.VMEM((wide, 2 * CHUNK), jnp.bfloat16),
            pltpu.VMEM((wide, 2 * CHUNK), jnp.bfloat16),
            pltpu.VMEM((2 * wide, 2 * CHUNK), jnp.bfloat16),
        ],
        compiler_params=pltpu.CompilerParams(
            dimension_semantics=("arbitrary",), vmem_limit_bytes=48 * 1024 * 1024
        ),
        cost_estimate=pl.CostEstimate(
            flops=8 * wide * wide * frequencies * 2,
            bytes_accessed=total * frequencies * 2 + 16 * wide * wide,
            transcendentals=0,
        ),
    )(arrived, unpack, cos, sin)


def local(spectra, fibre_lists, pairing):
    seg_all, held, _, frequencies = spectra.shape
    blk_count = lax.axis_size("blk")
    seg_count = lax.axis_size("seg")
    blk_index = lax.axis_index("blk")
    block_count, chan = fibre_lists.shape
    width = held * seg_count
    bound = 2 * (3 * chan // (2 * blk_count))
    partner = pairing[0]

    blocks = jnp.arange(block_count, dtype=jnp.int32)
    leads = assign(partner)
    owner = jnp.where(leads, blocks, partner) // 2
    lead_parity = (~leads[0::2]).astype(jnp.int32)
    lead = 2 * jnp.arange(blk_count, dtype=jnp.int32) + lead_parity
    follow = take_small(partner, lead)
    i32 = jnp.int32

    mine = blk_index * width + jnp.arange(width, dtype=i32)
    flat = fibre_lists.reshape(-1)
    flat_owner = jnp.repeat(owner, chan)
    pair_of = jnp.sum(jnp.where(flat[:, None] == mine[None, :], flat_owner[:, None], 0), axis=0)
    order = jnp.arange(width, dtype=i32)
    rank = jnp.sum((pair_of[:, None] == pair_of[None, :]) & (order[:, None] < order[None, :]), axis=0).astype(i32)
    spot = pair_of * bound + rank
    hit = jnp.arange(blk_count * bound, dtype=i32)[:, None] == spot[None, :]
    hit = hit.reshape(blk_count, 1, bound, seg_count, 1, held)
    part = jnp.arange(2, dtype=i32)
    same = (part[:, None] == part[None, :]).reshape(1, 2, 1, 1, 2, 1)
    pack = (hit & same).astype(jnp.bfloat16).reshape(blk_count * 2 * bound, 2 * width)

    pair = jnp.concatenate(
        [jnp.take(fibre_lists, lead[blk_index], axis=0), jnp.take(fibre_lists, follow[blk_index], axis=0)]
    )
    source = pair // width
    rank = jnp.sum((source[:, None] == source[None, :]) & (pair[None, :] < pair[:, None]), axis=1).astype(i32)
    spot = source * bound + rank
    hit = spot[:, None] == jnp.arange(blk_count * bound, dtype=i32)[None, :]
    hit = hit.reshape(1, 2 * chan, blk_count, 1, bound)
    same = (part[:, None] == part[None, :]).reshape(2, 1, 1, 2, 1)
    unpack = (hit & same).astype(jnp.bfloat16).reshape(4 * chan, blk_count * 2 * bound)

    rows = jnp.transpose(spectra, (0, 2, 1, 3)).reshape(seg_all, 2 * held, frequencies)
    column = lax.all_to_all(rows, "seg", split_axis=0, concat_axis=0, tiled=True)
    column = column.reshape(seg_count * 2 * held, frequencies)
    packed = jnp.dot(pack, column, preferred_element_type=jnp.float32).astype(jnp.bfloat16)
    packed = packed.reshape(blk_count, 2 * bound, frequencies)
    arrived = lax.all_to_all(packed, "blk", split_axis=0, concat_axis=0, tiled=True)
    plus, minus = correlate(arrived.reshape(blk_count * 2 * bound, frequencies), unpack, chan)

    share = chan // seg_count
    plus = plus.reshape(COARSE, seg_count, share, 2 * FINE * chan)
    minus = minus.reshape(2 * FINE, seg_count, share, COARSE * chan)
    both = jnp.stack(
        [
            jnp.transpose(plus, (1, 0, 2, 3)).reshape(seg_count, -1, chan),
            jnp.transpose(minus, (1, 0, 2, 3)).reshape(seg_count, -1, chan),
        ],
        axis=1,
    )
    kept = lax.psum_scatter(both, "seg", scatter_dimension=0, tiled=True)[0]
    scaling = 1.0 / math.sqrt(frequencies * seg_all)
    own = kept[0].reshape(COARSE, share, 2 * FINE, chan)
    own = jnp.transpose(own, (1, 3, 0, 2)).reshape(share, chan, LH) * scaling
    other = kept[1].reshape(2 * FINE, share, COARSE, chan)[::-1]
    other = jnp.transpose(other, (1, 3, 2, 0)).reshape(share, chan, LH) * scaling
    others = lax.all_gather(other, "blk", axis=0)
    lead_here = lead[blk_index]
    came_from = take_small(owner, (lead_here ^ 1)[None])[0]
    got = lax.dynamic_index_in_dim(others, came_from, 0, keepdims=False)
    first = lead_here % 2 == 0
    return jnp.stack([jnp.where(first, own, got), jnp.where(first, got, own)])[None]


def solution(mesh):
    in_specs = (P(None, ("blk", "seg"), None, None), P(), P())
    out_specs = P(None, "blk", "seg", None, None)
    return jax.shard_map(local, mesh=mesh, in_specs=in_specs, out_specs=out_specs, check_vma=False)
```

```python
import functools
import math

import numpy as np
import jax
import jax.numpy as jnp
from jax import lax
from jax.experimental import pallas as pl
from jax.experimental.pallas import tpu as pltpu
from jax.sharding import PartitionSpec as P

LH = 128
STEP = 16
COARSE = LH // STEP
FINE = STEP // 2
CHUNK = 512
NT = (((1,), (1,)), ((), ()))


def phase_tables(frequencies):
    freq = np.arange(frequencies, dtype=np.float64)[None, :]
    coarse = (STEP * np.arange(COARSE, dtype=np.float64) + (STEP - 1) / 2)[:, None]
    fine = (np.arange(FINE, dtype=np.float64) + 0.5)[:, None]
    angles = np.concatenate([coarse, fine], 0) * freq * (math.pi / frequencies)
    return np.cos(angles).astype(np.float32), np.sin(angles).astype(np.float32)


def take_small(table, index):
    hit = index[:, None] == jnp.arange(table.shape[0], dtype=jnp.int32)[None, :]
    return jnp.sum(jnp.where(hit, table[None, :], 0), axis=1)


def assign(partner):
    count = partner.shape[0]
    blocks = jnp.arange(count, dtype=jnp.int32)
    hop = partner ^ 1
    lowest = blocks
    for _ in range(max(1, (count // 2 - 1).bit_length())):
        lowest = jnp.minimum(lowest, take_small(lowest, hop))
        hop = take_small(hop, hop)
    return lowest < take_small(lowest, blocks ^ 1)


def fused_kernel(
    chan, bound, tail, rows_ref, pack, unpack, cos_ref, sin_ref, *rest
):
    if tail:
        own_ref, others_ref, *rest = rest
    else:
        plus_out, minus_out, *rest = rest
    col, packed, arr, xp, xm, yp, plus, minus, a_send, a_recv, b_send, b_recv, local_sem, *rest = rest
    blk_count, seg_count = lax.axis_size("blk"), lax.axis_size("seg")
    blk, seg = lax.axis_index("blk"), lax.axis_index("seg")
    chunks = col.shape[0]
    held = rows_ref.shape[1]
    width = col.shape[2]
    bf = jnp.bfloat16
    mesh_ids = pl.DeviceIdType.MESH

    def seg_peer(step):
        return lax.rem(seg + step, seg_count)

    def blk_peer(step):
        return lax.rem(blk + step, blk_count)

    barrier = pltpu.get_barrier_semaphore()
    for step in range(1, seg_count):
        pl.semaphore_signal(barrier, inc=1, device_id=(blk, seg_peer(step)), device_id_type=mesh_ids)
    for step in range(1, blk_count):
        pl.semaphore_signal(barrier, inc=1, device_id=(blk_peer(step), seg), device_id_type=mesh_ids)
    pl.semaphore_wait(barrier, seg_count + blk_count - 2)

    def a_copy(k, step):
        to = seg_peer(step)
        return pltpu.make_async_remote_copy(
            src_ref=rows_ref.at[to, :, pl.ds(pl.multiple_of(k * width, width), width)],
            dst_ref=col.at[k, pl.ds(pl.multiple_of(seg * held, held), held), :],
            send_sem=a_send.at[k, step],
            recv_sem=a_recv.at[k, step],
            device_id=(blk, to),
            device_id_type=mesh_ids,
        )

    def a_own(k):
        return pltpu.make_async_copy(
            rows_ref.at[seg, :, pl.ds(pl.multiple_of(k * width, width), width)],
            col.at[k, pl.ds(pl.multiple_of(seg * held, held), held), :],
            local_sem.at[k],
        )

    def b_copy(k, step):
        to = blk_peer(step)
        return pltpu.make_async_remote_copy(
            src_ref=packed.at[k, to],
            dst_ref=arr.at[k, blk],
            send_sem=b_send.at[k, step],
            recv_sem=b_recv.at[k, step],
            device_id=(to, seg),
            device_id_type=mesh_ids,
        )

    def b_own(k):
        return pltpu.make_async_copy(packed.at[k, blk], arr.at[k, blk], b_send.at[k, 0])

    @pl.loop(0, chunks)
    def _(k):
        for step in range(1, seg_count):
            a_copy(k, step).start()
        a_own(k).start()

    plus[...] = jnp.zeros_like(plus)
    minus[...] = jnp.zeros_like(minus)

    def route(k):
        for step in range(1, seg_count):
            a_copy(k, step).wait_recv()
        a_own(k).wait()
        mixed = jnp.dot(pack[...], col[k], preferred_element_type=jnp.float32).astype(bf)
        packed[k] = mixed.reshape(blk_count, 2 * bound, width)
        for step in range(1, blk_count):
            b_copy(k, step).start()
        b_own(k).start()

    def work(k):
        for step in range(1, blk_count):
            b_copy(k, step).wait_recv()
        b_own(k).wait()
        block = arr[k].reshape(blk_count * 2 * bound, width)
        rows = jnp.dot(unpack[...], block, preferred_element_type=jnp.float32)
        xr, yr = rows[0:chan], rows[chan : 2 * chan]
        xi, yi = rows[2 * chan : 3 * chan], rows[3 * chan : 4 * chan]
        re, im = pl.ds(0, width), pl.ds(width, width)
        for a in range(COARSE):
            c, s = cos_ref[k, a : a + 1, :], sin_ref[k, a : a + 1, :]
            rc, rs, ic, i_s = xr * c, xr * s, xi * c, xi * s
            at = pl.ds(a * chan, chan)
            xp[at, re] = (rc - i_s).astype(bf)
            xp[at, im] = (ic + rs).astype(bf)
            xm[at, re] = (rc + i_s).astype(bf)
            xm[at, im] = (ic - rs).astype(bf)
        for m in range(COARSE, COARSE + FINE):
            c, s = cos_ref[k, m : m + 1, :], sin_ref[k, m : m + 1, :]
            rc, rs, ic, i_s = yr * c, yr * s, yi * c, yi * s
            at, back = pl.ds((FINE + m - COARSE) * chan, chan), pl.ds((FINE - 1 - m + COARSE) * chan, chan)
            yp[at, re] = (rc + i_s).astype(bf)
            yp[at, im] = (ic - rs).astype(bf)
            yp[back, re] = (rc - i_s).astype(bf)
            yp[back, im] = (ic + rs).astype(bf)
        tile = 4 * chan

        @pl.loop(0, yp.shape[0] // tile)
        def _(t):
            at = pl.ds(pl.multiple_of(t * tile, tile), tile)
            y = yp[at, :]
            first = lax.dot_general(xp[...], y, NT, preferred_element_type=jnp.float32)
            plus[:, :, at] += first.reshape(COARSE, chan, tile)
            second = lax.dot_general(y, xm[...], NT, preferred_element_type=jnp.float32)
            minus[pl.ds(t * 4, 4)] += second.reshape(4, chan, COARSE * chan)

    route(0)

    @pl.loop(1, chunks)
    def _(k):
        route(k)
        work(k - 1)

    work(chunks - 1)

    if tail:
        from_core_m, from_core_p, stage_m, stage_p, from_z_m, from_z_p, done, c_send, c_recv, z_send, z_recv, o_send, o_recv, own_sem = rest
        share = chan // seg_count
        z_count = seg_count // 2
        core, z = lax.rem(seg, 2), lax.div(seg, 2)
        sides = ((minus, from_core_m, stage_m, from_z_m), (plus, from_core_p, stage_p, from_z_p))

        def z_peer(step):
            return lax.rem(z + step, z_count)

        def rows_of(target):
            return pl.ds(pl.multiple_of(target * share, share), share)

        def c_copy(side, step):
            acc, landing, _, _ = sides[side]
            to_z = z_peer(step)
            return pltpu.make_async_remote_copy(
                src_ref=acc.at[:, rows_of(2 * to_z + 1 - core), :],
                dst_ref=landing.at[step],
                send_sem=c_send.at[side, step],
                recv_sem=c_recv.at[side, step],
                device_id=(blk, 2 * z + 1 - core),
                device_id_type=mesh_ids,
            )

        def z_copy(side, step):
            _, _, stage, landing = sides[side]
            return pltpu.make_async_remote_copy(
                src_ref=stage.at[step],
                dst_ref=landing.at[step],
                send_sem=z_send.at[side, step],
                recv_sem=z_recv.at[side, step],
                device_id=(blk, 2 * z_peer(step) + core),
                device_id_type=mesh_ids,
            )

        order = list(range(1, z_count)) + [0]
        for side in range(2):
            for step in order:
                c_copy(side, step).start()
        for side in range(2):
            acc, landing, stage, _ = sides[side]
            for step in order[:-1]:
                c_copy(side, step).wait_recv()
                both = acc[:, rows_of(2 * z_peer(step) + core), :] + landing[step]
                stage[step] = both.reshape(-1, both.shape[-1]).astype(bf)
                z_copy(side, step).start()

        def finish(side):
            acc, landing, _, terms = sides[side]
            c_copy(side, 0).wait_recv()
            total = acc[:, rows_of(seg), :] + landing[0]
            for step in range(1, z_count):
                z_copy(side, step).wait_recv()
                total = total + terms[step].astype(jnp.float32).reshape(total.shape)
            return total

        def o_copy(step):
            return pltpu.make_async_remote_copy(
                src_ref=done,
                dst_ref=others_ref.at[blk],
                send_sem=o_send.at[step],
                recv_sem=o_recv.at[step],
                device_id=(blk_peer(step), seg),
                device_id_type=mesh_ids,
            )

        keep = pltpu.make_async_copy(done, others_ref.at[blk], own_sem)
        done[...] = finish(0)
        for step in range(1, blk_count):
            o_copy(step).start()
        keep.start()
        own_ref[...] = finish(1)
        keep.wait()
        for step in range(1, blk_count):
            o_copy(step).wait()
        for side in range(2):
            for step in order:
                c_copy(side, step).wait_send()
            for step in order[:-1]:
                z_copy(side, step).wait_send()
    else:
        plus_out[...] = plus[...]
        minus_out[...] = minus[...]

    @pl.loop(0, chunks)
    def _(k):
        for step in range(1, seg_count):
            a_copy(k, step).wait_send()
        for step in range(1, blk_count):
            b_copy(k, step).wait_send()


def correlate(rows, pack, unpack, chan, bound, tail):
    _, held, frequencies = rows.shape
    blk_count, seg_count = lax.axis_size("blk"), lax.axis_size("seg")
    chunks = frequencies // CHUNK
    cos, sin = phase_tables(frequencies)

    def by_chunk(table):
        return np.ascontiguousarray(table.reshape(-1, chunks, CHUNK).transpose(1, 0, 2))

    wide = COARSE * chan
    f32, bf = jnp.float32, jnp.bfloat16
    share = chan // seg_count
    z_count = seg_count // 2
    plus_shape, minus_shape = (COARSE, chan, 2 * wide), (2 * FINE, chan, wide)
    p_shape, m_shape = (COARSE, share, 2 * wide), (2 * FINE, share, wide)
    dma = pltpu.SemaphoreType.DMA
    in_vmem, anywhere = pl.BlockSpec(memory_space=pltpu.VMEM), pl.BlockSpec(memory_space=pl.ANY)
    scratch = [
        pltpu.VMEM((chunks, seg_count * held, CHUNK), bf),
        pltpu.VMEM((chunks, blk_count, 2 * bound, CHUNK), bf),
        pltpu.VMEM((chunks, blk_count, 2 * bound, CHUNK), bf),
        pltpu.VMEM((wide, 2 * CHUNK), bf),
        pltpu.VMEM((wide, 2 * CHUNK), bf),
        pltpu.VMEM((2 * wide, 2 * CHUNK), bf),
        pltpu.VMEM(plus_shape, f32),
        pltpu.VMEM(minus_shape, f32),
        dma((chunks, seg_count)),
        dma((chunks, seg_count)),
        dma((chunks, blk_count)),
        dma((chunks, blk_count)),
        dma((chunks,)),
    ]
    if tail:
        out_shape = [jax.ShapeDtypeStruct(p_shape, f32), jax.ShapeDtypeStruct((blk_count,) + m_shape, f32)]
        out_specs = [in_vmem, anywhere]
        flat_p, flat_m = (COARSE * share, 2 * wide), (2 * FINE * share, wide)
        scratch += [
            pltpu.VMEM((z_count,) + m_shape, f32),
            pltpu.VMEM((z_count,) + p_shape, f32),
            pltpu.VMEM((z_count,) + flat_m, bf),
            pltpu.VMEM((z_count,) + flat_p, bf),
            pltpu.VMEM((z_count,) + flat_m, bf),
            pltpu.VMEM((z_count,) + flat_p, bf),
            pltpu.VMEM(m_shape, f32),
            dma((2, z_count)),
            dma((2, z_count)),
            dma((2, z_count)),
            dma((2, z_count)),
            dma((blk_count,)),
            dma((blk_count,)),
            dma(()),
        ]
    else:
        out_shape = [jax.ShapeDtypeStruct(plus_shape, f32), jax.ShapeDtypeStruct(minus_shape, f32)]
        out_specs = [in_vmem, in_vmem]
    return pl.pallas_call(
        functools.partial(fused_kernel, chan, bound, tail),
        in_specs=[anywhere] + [in_vmem] * 4,
        out_specs=out_specs,
        out_shape=out_shape,
        scratch_shapes=scratch,
        compiler_params=pltpu.CompilerParams(
            collective_id=0, has_side_effects=True, vmem_limit_bytes=56 * 1024 * 1024
        ),
        cost_estimate=pl.CostEstimate(
            flops=8 * wide * wide * frequencies * 2, bytes_accessed=16 * wide * wide, transcendentals=0
        ),
    )(rows, pack, unpack, by_chunk(cos), by_chunk(sin))


def local(spectra, fibre_lists, pairing):
    seg_all, held, _, frequencies = spectra.shape
    blk_count = lax.axis_size("blk")
    seg_count = lax.axis_size("seg")
    blk_index = lax.axis_index("blk")
    block_count, chan = fibre_lists.shape
    width = held * seg_count
    bound = 2 * (3 * chan // (2 * blk_count))
    partner = pairing[0]

    blocks = jnp.arange(block_count, dtype=jnp.int32)
    leads = assign(partner)
    owner = jnp.where(leads, blocks, partner) // 2
    lead_parity = (~leads[0::2]).astype(jnp.int32)
    lead = 2 * jnp.arange(blk_count, dtype=jnp.int32) + lead_parity
    follow = take_small(partner, lead)
    i32 = jnp.int32

    mine = blk_index * width + jnp.arange(width, dtype=i32)
    flat = fibre_lists.reshape(-1)
    flat_owner = jnp.repeat(owner, chan)
    pair_of = jnp.sum(jnp.where(flat[:, None] == mine[None, :], flat_owner[:, None], 0), axis=0)
    order = jnp.arange(width, dtype=i32)
    rank = jnp.sum((pair_of[:, None] == pair_of[None, :]) & (order[:, None] < order[None, :]), axis=0).astype(i32)
    spot = pair_of * bound + rank
    hit = jnp.arange(blk_count * bound, dtype=i32)[:, None] == spot[None, :]
    hit = hit.reshape(blk_count, 1, bound, seg_count, 1, held)
    part = jnp.arange(2, dtype=i32)
    same = (part[:, None] == part[None, :]).reshape(1, 2, 1, 1, 2, 1)
    pack = (hit & same).astype(jnp.bfloat16).reshape(blk_count * 2 * bound, 2 * width)

    pair = jnp.concatenate(
        [jnp.take(fibre_lists, lead[blk_index], axis=0), jnp.take(fibre_lists, follow[blk_index], axis=0)]
    )
    source = pair // width
    rank = jnp.sum((source[:, None] == source[None, :]) & (pair[None, :] < pair[:, None]), axis=1).astype(i32)
    spot = source * bound + rank
    hit = spot[:, None] == jnp.arange(blk_count * bound, dtype=i32)[None, :]
    hit = hit.reshape(1, 2 * chan, blk_count, 1, bound)
    same = (part[:, None] == part[None, :]).reshape(2, 1, 1, 2, 1)
    unpack = (hit & same).astype(jnp.bfloat16).reshape(4 * chan, blk_count * 2 * bound)

    rows = jnp.transpose(spectra, (0, 2, 1, 3)).reshape(seg_all, 2 * held, frequencies)
    share = chan // seg_count
    tail = share % 8 == 0
    plus, minus = correlate(rows, pack, unpack, chan, bound, tail)
    lead_here = lead[blk_index]
    came_from = take_small(owner, (lead_here ^ 1)[None])[0]
    scaling = 1.0 / math.sqrt(frequencies * seg_all)
    if tail:
        other = lax.dynamic_index_in_dim(minus, came_from, 0, keepdims=False)
    else:
        plus = lax.psum_scatter(plus, "seg", scatter_dimension=1, tiled=True)
        other = lax.psum_scatter(minus, "seg", scatter_dimension=1, tiled=True)
        others = lax.all_gather(other, "blk", axis=0)
        other = lax.dynamic_index_in_dim(others, came_from, 0, keepdims=False)
    own = plus.reshape(COARSE, share, 2 * FINE, chan)
    own = jnp.transpose(own, (1, 3, 0, 2)).reshape(share, chan, LH) * scaling
    got = other.reshape(2 * FINE, share, COARSE, chan)[::-1]
    got = jnp.transpose(got, (1, 3, 2, 0)).reshape(share, chan, LH) * scaling
    first = lead_here % 2 == 0
    return jnp.stack([jnp.where(first, own, got), jnp.where(first, got, own)])[None]


def solution(mesh):
    in_specs = (P(None, ("blk", "seg"), None, None), P(), P())
    out_specs = P(None, "blk", "seg", None, None)
    return jax.shard_map(local, mesh=mesh, in_specs=in_specs, out_specs=out_specs, check_vma=False)
```

```python
import functools
import math

import numpy as np
import jax
import jax.numpy as jnp
from jax import lax
from jax.experimental import pallas as pl
from jax.experimental.pallas import tpu as pltpu
from jax.sharding import PartitionSpec as P

LH = 128
STEP = 16
COARSE = LH // STEP
FINE = STEP // 2
CHUNK = 512
NT = (((1,), (1,)), ((), ()))


def phase_tables(frequencies):
    freq = np.arange(frequencies, dtype=np.float64)[None, :]
    coarse = (STEP * np.arange(COARSE, dtype=np.float64) + (STEP - 1) / 2)[:, None]
    fine = (np.arange(FINE, dtype=np.float64) + 0.5)[:, None]
    angles = np.concatenate([coarse, fine], 0) * freq * (math.pi / frequencies)
    return np.cos(angles).astype(np.float32), np.sin(angles).astype(np.float32)


def plan(chan, bound, width, blk, blk_count, pairing, lists, lists_t, places, pack, unpack, chosen):
    count = lists.shape[0]
    i32, f32, bf = jnp.int32, jnp.float32, jnp.bfloat16

    def lowest(block):
        least = block
        at = block
        for _ in range(count // 2 - 1):
            at = pairing[0, at] ^ 1
            least = jnp.minimum(least, at)
        return least

    least = [lowest(jnp.int32(b)) for b in range(count)]
    owner = [
        jnp.where(least[b] < least[b ^ 1], jnp.int32(b), pairing[0, b]) // 2 for b in range(count)
    ]
    lead = jnp.int32(0)
    came_from = jnp.int32(0)
    for k in range(blk_count):
        first = least[2 * k] < least[2 * k + 1]
        lead = jnp.where(blk == k, jnp.where(first, 2 * k, 2 * k + 1), lead)
        came_from = jnp.where(blk == k, jnp.where(first, owner[2 * k + 1], owner[2 * k]), came_from)
    follow = pairing[0, lead]
    chosen[0] = came_from
    chosen[1] = lead % 2

    columns = places.shape[1]
    number = places[0:1, :]
    pair_of = jnp.zeros((1, columns), i32)
    for b in range(count):
        hit = lists_t[:, b : b + 1] == number + blk * width
        pair_of = pair_of + jnp.sum(jnp.where(hit, owner[b], 0), axis=0, keepdims=True)
    kinds = max(8, blk_count)
    real = (lax.broadcasted_iota(i32, (kinds, columns), 0) == pair_of) & (places[1:2, :] == 0)
    before = places[2 : 2 + columns, :] < number
    ranks = jnp.dot(
        jnp.where(real, 1.0, 0.0).astype(bf),
        jnp.where(before, 1.0, 0.0).astype(bf),
        preferred_element_type=f32,
    )
    mine = lax.broadcasted_iota(i32, (kinds, columns), 0) == pair_of
    rank = jnp.sum(jnp.where(mine, ranks, 0.0), axis=0, keepdims=True).astype(i32)
    target = pair_of * (2 * bound) + places[1:2, :] * bound + rank
    pack[...] = jnp.where(lax.broadcasted_iota(i32, pack.shape, 0) == target, 1.0, 0.0).astype(bf)

    roles = (lead, follow)
    zero_col, zero_row = jnp.zeros((chan, 1), i32), jnp.zeros((1, chan), i32)
    tall = [sum((jnp.where(role == b, lists_t[:, b : b + 1], 0) for b in range(count)), zero_col) for role in roles]
    flat = [sum((jnp.where(role == b, lists[b : b + 1, :], 0) for b in range(count)), zero_row) for role in roles]
    shift = width.bit_length() - 1
    lane = lax.broadcasted_iota(i32, (chan, unpack.shape[1]), 1)
    for r in range(2):
        rank = zero_col
        for other in flat:
            ahead = ((tall[r] >> shift) == (other >> shift)) & (other < tall[r])
            rank = rank + jnp.sum(jnp.where(ahead, 1, 0), axis=1, keepdims=True)
        spot = (tall[r] >> shift) * (2 * bound) + rank
        for part in range(2):
            hit = lane == spot + part * bound
            unpack[(2 * part + r) * chan : (2 * part + r + 1) * chan, :] = jnp.where(hit, 1.0, 0.0).astype(bf)


def fused_kernel(
    chan, bound, tail, rows_ref, pairing, lists, lists_t, places, cos_ref, sin_ref, *rest
):
    if tail:
        own_ref, others_ref, chosen, *rest = rest
    else:
        plus_out, minus_out, chosen, *rest = rest
    pack, unpack, col, packed, arr, xp, xm, yp, plus, minus, a_send, a_recv, b_send, b_recv, local_sem, *rest = rest
    blk_count, seg_count = lax.axis_size("blk"), lax.axis_size("seg")
    blk, seg = lax.axis_index("blk"), lax.axis_index("seg")
    chunks = col.shape[0]
    held = rows_ref.shape[1]
    width = col.shape[2]
    bf = jnp.bfloat16
    mesh_ids = pl.DeviceIdType.MESH

    def seg_peer(step):
        return lax.rem(seg + step, seg_count)

    def blk_peer(step):
        return lax.rem(blk + step, blk_count)

    barrier = pltpu.get_barrier_semaphore()
    for step in range(1, seg_count):
        pl.semaphore_signal(barrier, inc=1, device_id=(blk, seg_peer(step)), device_id_type=mesh_ids)
    for step in range(1, blk_count):
        pl.semaphore_signal(barrier, inc=1, device_id=(blk_peer(step), seg), device_id_type=mesh_ids)
    pl.semaphore_wait(barrier, seg_count + blk_count - 2)

    def a_copy(k, step):
        to = seg_peer(step)
        return pltpu.make_async_remote_copy(
            src_ref=rows_ref.at[to, :, pl.ds(pl.multiple_of(k * width, width), width)],
            dst_ref=col.at[k, pl.ds(pl.multiple_of(seg * held, held), held), :],
            send_sem=a_send.at[k, step],
            recv_sem=a_recv.at[k, step],
            device_id=(blk, to),
            device_id_type=mesh_ids,
        )

    def a_own(k):
        return pltpu.make_async_copy(
            rows_ref.at[seg, :, pl.ds(pl.multiple_of(k * width, width), width)],
            col.at[k, pl.ds(pl.multiple_of(seg * held, held), held), :],
            local_sem.at[k],
        )

    def b_copy(k, step):
        to = blk_peer(step)
        return pltpu.make_async_remote_copy(
            src_ref=packed.at[k, to],
            dst_ref=arr.at[k, blk],
            send_sem=b_send.at[k, step],
            recv_sem=b_recv.at[k, step],
            device_id=(to, seg),
            device_id_type=mesh_ids,
        )

    def b_own(k):
        return pltpu.make_async_copy(packed.at[k, blk], arr.at[k, blk], b_send.at[k, 0])

    @pl.loop(0, chunks)
    def _(k):
        for step in range(1, seg_count):
            a_copy(k, step).start()
        a_own(k).start()

    plus[...] = jnp.zeros_like(plus)
    minus[...] = jnp.zeros_like(minus)
    plan(chan, bound, seg_count * held // 2, blk, blk_count, pairing, lists, lists_t, places, pack, unpack, chosen)

    def route(k):
        for step in range(1, seg_count):
            a_copy(k, step).wait_recv()
        a_own(k).wait()
        mixed = jnp.dot(pack[...], col[k], preferred_element_type=jnp.float32).astype(bf)
        packed[k] = mixed.reshape(blk_count, 2 * bound, width)
        for step in range(1, blk_count):
            b_copy(k, step).start()
        b_own(k).start()

    def work(k):
        for step in range(1, blk_count):
            b_copy(k, step).wait_recv()
        b_own(k).wait()
        block = arr[k].reshape(blk_count * 2 * bound, width)
        rows = jnp.dot(unpack[...], block, preferred_element_type=jnp.float32)
        xr, yr = rows[0:chan], rows[chan : 2 * chan]
        xi, yi = rows[2 * chan : 3 * chan], rows[3 * chan : 4 * chan]
        re, im = pl.ds(0, width), pl.ds(width, width)
        for a in range(COARSE):
            c, s = cos_ref[k, a : a + 1, :], sin_ref[k, a : a + 1, :]
            rc, rs, ic, i_s = xr * c, xr * s, xi * c, xi * s
            at = pl.ds(a * chan, chan)
            xp[at, re] = (rc - i_s).astype(bf)
            xp[at, im] = (ic + rs).astype(bf)
            xm[at, re] = (rc + i_s).astype(bf)
            xm[at, im] = (ic - rs).astype(bf)
        for m in range(COARSE, COARSE + FINE):
            c, s = cos_ref[k, m : m + 1, :], sin_ref[k, m : m + 1, :]
            rc, rs, ic, i_s = yr * c, yr * s, yi * c, yi * s
            at, back = pl.ds((FINE + m - COARSE) * chan, chan), pl.ds((FINE - 1 - m + COARSE) * chan, chan)
            yp[at, re] = (rc + i_s).astype(bf)
            yp[at, im] = (ic - rs).astype(bf)
            yp[back, re] = (rc - i_s).astype(bf)
            yp[back, im] = (ic + rs).astype(bf)
        tile = 4 * chan

        @pl.loop(0, yp.shape[0] // tile)
        def _(t):
            at = pl.ds(pl.multiple_of(t * tile, tile), tile)
            y = yp[at, :]
            first = lax.dot_general(xp[...], y, NT, preferred_element_type=jnp.float32)
            plus[:, :, at] += first.reshape(COARSE, chan, tile)
            second = lax.dot_general(y, xm[...], NT, preferred_element_type=jnp.float32)
            minus[pl.ds(t * 4, 4)] += second.reshape(4, chan, COARSE * chan)

    route(0)

    @pl.loop(1, chunks)
    def _(k):
        route(k)
        work(k - 1)

    work(chunks - 1)

    if tail:
        from_core_m, from_core_p, stage_m, stage_p, from_z_m, from_z_p, done, c_send, c_recv, z_send, z_recv, o_send, o_recv, own_sem = rest
        share = chan // seg_count
        z_count = seg_count // 2
        core, z = lax.rem(seg, 2), lax.div(seg, 2)
        sides = ((minus, from_core_m, stage_m, from_z_m), (plus, from_core_p, stage_p, from_z_p))

        def z_peer(step):
            return lax.rem(z + step, z_count)

        def rows_of(target):
            return pl.ds(pl.multiple_of(target * share, share), share)

        def c_copy(side, step):
            acc, landing, _, _ = sides[side]
            to_z = z_peer(step)
            return pltpu.make_async_remote_copy(
                src_ref=acc.at[:, rows_of(2 * to_z + 1 - core), :],
                dst_ref=landing.at[step],
                send_sem=c_send.at[side, step],
                recv_sem=c_recv.at[side, step],
                device_id=(blk, 2 * z + 1 - core),
                device_id_type=mesh_ids,
            )

        def z_copy(side, step):
            _, _, stage, landing = sides[side]
            return pltpu.make_async_remote_copy(
                src_ref=stage.at[step],
                dst_ref=landing.at[step],
                send_sem=z_send.at[side, step],
                recv_sem=z_recv.at[side, step],
                device_id=(blk, 2 * z_peer(step) + core),
                device_id_type=mesh_ids,
            )

        order = list(range(1, z_count)) + [0]
        for side in range(2):
            for step in order:
                c_copy(side, step).start()
        for side in range(2):
            acc, landing, stage, _ = sides[side]
            for step in order[:-1]:
                c_copy(side, step).wait_recv()
                both = acc[:, rows_of(2 * z_peer(step) + core), :] + landing[step]
                stage[step] = both.reshape(-1, both.shape[-1]).astype(bf)
                z_copy(side, step).start()

        def finish(side):
            acc, landing, _, terms = sides[side]
            c_copy(side, 0).wait_recv()
            total = acc[:, rows_of(seg), :] + landing[0]
            for step in range(1, z_count):
                z_copy(side, step).wait_recv()
                total = total + terms[step].astype(jnp.float32).reshape(total.shape)
            return total

        def o_copy(step):
            return pltpu.make_async_remote_copy(
                src_ref=done,
                dst_ref=others_ref.at[blk],
                send_sem=o_send.at[step],
                recv_sem=o_recv.at[step],
                device_id=(blk_peer(step), seg),
                device_id_type=mesh_ids,
            )

        keep = pltpu.make_async_copy(done, others_ref.at[blk], own_sem)
        done[...] = finish(0)
        for step in range(1, blk_count):
            o_copy(step).start()
        keep.start()
        own_ref[...] = finish(1)
        keep.wait()
        for step in range(1, blk_count):
            o_copy(step).wait()
        for side in range(2):
            for step in order:
                c_copy(side, step).wait_send()
            for step in order[:-1]:
                z_copy(side, step).wait_send()
    else:
        plus_out[...] = plus[...]
        minus_out[...] = minus[...]

    @pl.loop(0, chunks)
    def _(k):
        for step in range(1, seg_count):
            a_copy(k, step).wait_send()
        for step in range(1, blk_count):
            b_copy(k, step).wait_send()


def correlate(rows, pairing, fibre_lists, bound, tail):
    held, frequencies = rows.shape[1], rows.shape[2]
    chan = fibre_lists.shape[1]
    blk_count, seg_count = lax.axis_size("blk"), lax.axis_size("seg")
    chunks = frequencies // CHUNK
    cos, sin = phase_tables(frequencies)

    def by_chunk(table):
        return np.ascontiguousarray(table.reshape(-1, chunks, CHUNK).transpose(1, 0, 2))

    slots = np.arange(seg_count * held)
    number = slots // held * (held // 2) + slots % (held // 2)
    part = slots // (held // 2) % 2
    across = np.broadcast_to(number[:, None], (slots.size, slots.size))
    places = np.concatenate([number[None], part[None], across]).astype(np.int32)

    wide = COARSE * chan
    f32, bf = jnp.float32, jnp.bfloat16
    share = chan // seg_count
    z_count = seg_count // 2
    plus_shape, minus_shape = (COARSE, chan, 2 * wide), (2 * FINE, chan, wide)
    p_shape, m_shape = (COARSE, share, 2 * wide), (2 * FINE, share, wide)
    dma = pltpu.SemaphoreType.DMA
    in_vmem, anywhere = pl.BlockSpec(memory_space=pltpu.VMEM), pl.BlockSpec(memory_space=pl.ANY)
    in_smem, picked = pl.BlockSpec(memory_space=pltpu.SMEM), jax.ShapeDtypeStruct((2,), jnp.int32)
    scratch = [
        pltpu.VMEM((blk_count * 2 * bound, seg_count * held), bf),
        pltpu.VMEM((4 * chan, blk_count * 2 * bound), bf),
        pltpu.VMEM((chunks, seg_count * held, CHUNK), bf),
        pltpu.VMEM((chunks, blk_count, 2 * bound, CHUNK), bf),
        pltpu.VMEM((chunks, blk_count, 2 * bound, CHUNK), bf),
        pltpu.VMEM((wide, 2 * CHUNK), bf),
        pltpu.VMEM((wide, 2 * CHUNK), bf),
        pltpu.VMEM((2 * wide, 2 * CHUNK), bf),
        pltpu.VMEM(plus_shape, f32),
        pltpu.VMEM(minus_shape, f32),
        dma((chunks, seg_count)),
        dma((chunks, seg_count)),
        dma((chunks, blk_count)),
        dma((chunks, blk_count)),
        dma((chunks,)),
    ]
    if tail:
        out_shape = [jax.ShapeDtypeStruct(p_shape, f32), jax.ShapeDtypeStruct((blk_count,) + m_shape, f32), picked]
        out_specs = [in_vmem, anywhere, in_smem]
        flat_p, flat_m = (COARSE * share, 2 * wide), (2 * FINE * share, wide)
        scratch += [
            pltpu.VMEM((z_count,) + m_shape, f32),
            pltpu.VMEM((z_count,) + p_shape, f32),
            pltpu.VMEM((z_count,) + flat_m, bf),
            pltpu.VMEM((z_count,) + flat_p, bf),
            pltpu.VMEM((z_count,) + flat_m, bf),
            pltpu.VMEM((z_count,) + flat_p, bf),
            pltpu.VMEM(m_shape, f32),
            dma((2, z_count)),
            dma((2, z_count)),
            dma((2, z_count)),
            dma((2, z_count)),
            dma((blk_count,)),
            dma((blk_count,)),
            dma(()),
        ]
    else:
        out_shape = [jax.ShapeDtypeStruct(plus_shape, f32), jax.ShapeDtypeStruct(minus_shape, f32), picked]
        out_specs = [in_vmem, in_vmem, in_smem]
    return pl.pallas_call(
        functools.partial(fused_kernel, chan, bound, tail),
        in_specs=[anywhere, in_smem] + [in_vmem] * 5,
        out_specs=out_specs,
        out_shape=out_shape,
        scratch_shapes=scratch,
        compiler_params=pltpu.CompilerParams(
            collective_id=0, has_side_effects=True, vmem_limit_bytes=56 * 1024 * 1024
        ),
        cost_estimate=pl.CostEstimate(
            flops=8 * wide * wide * frequencies * 2, bytes_accessed=16 * wide * wide, transcendentals=0
        ),
    )(rows, pairing, fibre_lists, fibre_lists.T, places, by_chunk(cos), by_chunk(sin))


def local(spectra, fibre_lists, pairing):
    seg_all, held, _, frequencies = spectra.shape
    blk_count, seg_count = lax.axis_size("blk"), lax.axis_size("seg")
    chan = fibre_lists.shape[1]
    bound = 2 * (3 * chan // (2 * blk_count))

    rows = jnp.transpose(spectra, (0, 2, 1, 3)).reshape(seg_all, 2 * held, frequencies)
    share = chan // seg_count
    tail = share % 8 == 0
    plus, minus, chosen = correlate(rows, pairing, fibre_lists, bound, tail)
    came_from = chosen[0]
    scaling = 1.0 / math.sqrt(frequencies * seg_all)
    if tail:
        other = lax.dynamic_index_in_dim(minus, came_from, 0, keepdims=False)
    else:
        plus = lax.psum_scatter(plus, "seg", scatter_dimension=1, tiled=True)
        other = lax.psum_scatter(minus, "seg", scatter_dimension=1, tiled=True)
        others = lax.all_gather(other, "blk", axis=0)
        other = lax.dynamic_index_in_dim(others, came_from, 0, keepdims=False)
    own = plus.reshape(COARSE, share, 2 * FINE, chan)
    own = jnp.transpose(own, (1, 3, 0, 2)).reshape(share, chan, LH) * scaling
    got = other.reshape(2 * FINE, share, COARSE, chan)[::-1]
    got = jnp.transpose(got, (1, 3, 2, 0)).reshape(share, chan, LH) * scaling
    first = chosen[1] == 0
    return jnp.stack([jnp.where(first, own, got), jnp.where(first, got, own)])[None]


def solution(mesh):
    in_specs = (P(None, ("blk", "seg"), None, None), P(), P())
    out_specs = P(None, "blk", "seg", None, None)
    return jax.shard_map(local, mesh=mesh, in_specs=in_specs, out_specs=out_specs, check_vma=False)
```

```python
import functools
import math

import numpy as np
import jax
import jax.numpy as jnp
from jax import lax
from jax.experimental import pallas as pl
from jax.experimental.pallas import tpu as pltpu
from jax.sharding import PartitionSpec as P

LH = 128
STEP = 16
COARSE = LH // STEP
FINE = STEP // 2
CHUNK = 256
NT = (((1,), (1,)), ((), ()))


def phase_tables(frequencies):
    freq = np.arange(frequencies, dtype=np.float64)[None, :]
    coarse = (STEP * np.arange(COARSE, dtype=np.float64) + (STEP - 1) / 2)[:, None]
    fine = (np.arange(FINE, dtype=np.float64) + 0.5)[:, None]
    angles = np.concatenate([coarse, fine], 0) * freq * (math.pi / frequencies)
    return np.cos(angles).astype(np.float32), np.sin(angles).astype(np.float32)


def plan(chan, bound, width, blk, blk_count, pairing, lists, places, pack, unpack):
    count = lists.shape[0]
    lists_t = jnp.swapaxes(lists[...], 0, 1)
    i32, f32, bf = jnp.int32, jnp.float32, jnp.bfloat16

    def lowest(block):
        least = block
        at = block
        for _ in range(count // 2 - 1):
            at = pairing[0, at] ^ 1
            least = jnp.minimum(least, at)
        return least

    least = [lowest(jnp.int32(b)) for b in range(count)]
    owner = [
        jnp.where(least[b] < least[b ^ 1], jnp.int32(b), pairing[0, b]) // 2 for b in range(count)
    ]
    lead = jnp.int32(0)
    came_from = jnp.int32(0)
    for k in range(blk_count):
        first = least[2 * k] < least[2 * k + 1]
        lead = jnp.where(blk == k, jnp.where(first, 2 * k, 2 * k + 1), lead)
        came_from = jnp.where(blk == k, jnp.where(first, owner[2 * k + 1], owner[2 * k]), came_from)
    follow = pairing[0, lead]

    columns = places.shape[1]
    number = places[0:1, :]
    pair_of = jnp.zeros((1, columns), i32)
    for b in range(count):
        hit = lists_t[:, b : b + 1] == number + blk * width
        pair_of = pair_of + jnp.sum(jnp.where(hit, owner[b], 0), axis=0, keepdims=True)
    kinds = max(8, blk_count)
    real = (lax.broadcasted_iota(i32, (kinds, columns), 0) == pair_of) & (places[1:2, :] == 0)
    before = places[2 : 2 + columns, :] < number
    ranks = jnp.dot(
        jnp.where(real, 1.0, 0.0).astype(bf),
        jnp.where(before, 1.0, 0.0).astype(bf),
        preferred_element_type=f32,
    )
    mine = lax.broadcasted_iota(i32, (kinds, columns), 0) == pair_of
    rank = jnp.sum(jnp.where(mine, ranks, 0.0), axis=0, keepdims=True).astype(i32)
    target = pair_of * (2 * bound) + places[1:2, :] * bound + rank
    pack[...] = jnp.where(lax.broadcasted_iota(i32, pack.shape, 0) == target, 1.0, 0.0).astype(bf)

    roles = (lead, follow)
    zero_col, zero_row = jnp.zeros((chan, 1), i32), jnp.zeros((1, chan), i32)
    tall = [sum((jnp.where(role == b, lists_t[:, b : b + 1], 0) for b in range(count)), zero_col) for role in roles]
    flat = [sum((jnp.where(role == b, lists[b : b + 1, :], 0) for b in range(count)), zero_row) for role in roles]
    shift = width.bit_length() - 1
    lane = lax.broadcasted_iota(i32, (chan, unpack.shape[1]), 1)
    for r in range(2):
        rank = zero_col
        for other in flat:
            ahead = ((tall[r] >> shift) == (other >> shift)) & (other < tall[r])
            rank = rank + jnp.sum(jnp.where(ahead, 1, 0), axis=1, keepdims=True)
        spot = (tall[r] >> shift) * (2 * bound) + rank
        for part in range(2):
            hit = lane == spot + part * bound
            unpack[(2 * part + r) * chan : (2 * part + r + 1) * chan, :] = jnp.where(hit, 1.0, 0.0).astype(bf)
    return came_from, lead & 1


def lag_order(blocks):
    return jnp.swapaxes(jnp.swapaxes(jnp.stack(blocks), 0, 1), 1, 2)


def fused_kernel(
    chan, bound, tail, scaling, rows_ref, pairing, lists, places, cos_ref, sin_ref, *rest
):
    if tail:
        out_ref, *rest = rest
    else:
        plus_out, minus_out, picks_out, *rest = rest
    pack, unpack, col, packed, arr, xp, xm, yp, plus, minus, a_send, a_recv, b_send, b_recv, local_sem, *rest = rest
    blk_count, seg_count = lax.axis_size("blk"), lax.axis_size("seg")
    blk, seg = lax.axis_index("blk"), lax.axis_index("seg")
    chunks = col.shape[0]
    held = rows_ref.shape[1]
    width = col.shape[2]
    bf = jnp.bfloat16
    mesh_ids = pl.DeviceIdType.MESH

    def seg_peer(step):
        return lax.rem(seg + step, seg_count)

    def blk_peer(step):
        return lax.rem(blk + step, blk_count)

    barrier = pltpu.get_barrier_semaphore()
    for step in range(1, seg_count):
        pl.semaphore_signal(barrier, inc=1, device_id=(blk, seg_peer(step)), device_id_type=mesh_ids)
    for step in range(1, blk_count):
        pl.semaphore_signal(barrier, inc=1, device_id=(blk_peer(step), seg), device_id_type=mesh_ids)
    pl.semaphore_wait(barrier, seg_count + blk_count - 2)

    def a_copy(k, step):
        to = seg_peer(step)
        return pltpu.make_async_remote_copy(
            src_ref=rows_ref.at[to, :, pl.ds(pl.multiple_of(k * width, width), width)],
            dst_ref=col.at[k, pl.ds(pl.multiple_of(seg * held, held), held), :],
            send_sem=a_send.at[k, step],
            recv_sem=a_recv.at[k, step],
            device_id=(blk, to),
            device_id_type=mesh_ids,
        )

    def a_own(k):
        return pltpu.make_async_copy(
            rows_ref.at[seg, :, pl.ds(pl.multiple_of(k * width, width), width)],
            col.at[k, pl.ds(pl.multiple_of(seg * held, held), held), :],
            local_sem.at[k],
        )

    def b_copy(k, step):
        to = blk_peer(step)
        return pltpu.make_async_remote_copy(
            src_ref=packed.at[k, to],
            dst_ref=arr.at[k, blk],
            send_sem=b_send.at[k, step],
            recv_sem=b_recv.at[k, step],
            device_id=(to, seg),
            device_id_type=mesh_ids,
        )

    def b_own(k):
        return pltpu.make_async_copy(packed.at[k, blk], arr.at[k, blk], b_send.at[k, 0])

    @pl.loop(0, chunks)
    def _(k):
        for step in range(1, seg_count):
            a_copy(k, step).start()
        a_own(k).start()

    plus[...] = jnp.zeros_like(plus)
    minus[...] = jnp.zeros_like(minus)
    came_from, parity = plan(chan, bound, seg_count * held // 2, blk, blk_count, pairing, lists, places, pack, unpack)

    def route(k):
        for step in range(1, seg_count):
            a_copy(k, step).wait_recv()
        a_own(k).wait()
        mixed = jnp.dot(pack[...], col[k], preferred_element_type=jnp.float32).astype(bf)
        packed[k] = mixed.reshape(blk_count, 2 * bound, width)
        for step in range(1, blk_count):
            b_copy(k, step).start()
        b_own(k).start()

    def work(k):
        for step in range(1, blk_count):
            b_copy(k, step).wait_recv()
        b_own(k).wait()
        block = arr[k].reshape(blk_count * 2 * bound, width)
        rows = jnp.dot(unpack[...], block, preferred_element_type=jnp.float32)
        xr, yr = rows[0:chan], rows[chan : 2 * chan]
        xi, yi = rows[2 * chan : 3 * chan], rows[3 * chan : 4 * chan]
        re, im = pl.ds(0, width), pl.ds(width, width)
        for a in range(COARSE):
            c, s = cos_ref[k, a : a + 1, :], sin_ref[k, a : a + 1, :]
            rc, rs, ic, i_s = xr * c, xr * s, xi * c, xi * s
            at = pl.ds(a * chan, chan)
            xp[at, re] = (rc - i_s).astype(bf)
            xp[at, im] = (ic + rs).astype(bf)
            xm[at, re] = (rc + i_s).astype(bf)
            xm[at, im] = (ic - rs).astype(bf)
        for m in range(COARSE, COARSE + FINE):
            c, s = cos_ref[k, m : m + 1, :], sin_ref[k, m : m + 1, :]
            rc, rs, ic, i_s = yr * c, yr * s, yi * c, yi * s
            at, back = pl.ds((FINE + m - COARSE) * chan, chan), pl.ds((FINE - 1 - m + COARSE) * chan, chan)
            yp[at, re] = (rc + i_s).astype(bf)
            yp[at, im] = (ic - rs).astype(bf)
            yp[back, re] = (rc - i_s).astype(bf)
            yp[back, im] = (ic + rs).astype(bf)
        tile = 4 * chan

        @pl.loop(0, yp.shape[0] // tile)
        def _(t):
            at = pl.ds(pl.multiple_of(t * tile, tile), tile)
            y = yp[at, :]
            first = lax.dot_general(xp[...], y, NT, preferred_element_type=jnp.float32)
            plus[:, :, at] += first.reshape(COARSE, chan, tile)
            second = lax.dot_general(y, xm[...], NT, preferred_element_type=jnp.float32)
            minus[pl.ds(t * 4, 4)] += second.reshape(4, chan, COARSE * chan)

    route(0)

    @pl.loop(1, chunks)
    def _(k):
        route(k)
        work(k - 1)

    work(chunks - 1)

    if tail:
        from_core_m, from_core_p, stage_m, stage_p, from_z_m, from_z_p, done, others_ref, c_send, c_recv, z_send, z_recv, o_send, o_recv, own_sem = rest
        share = chan // seg_count
        z_count = seg_count // 2
        core, z = lax.rem(seg, 2), lax.div(seg, 2)
        sides = ((minus, from_core_m, stage_m, from_z_m), (plus, from_core_p, stage_p, from_z_p))

        def z_peer(step):
            return lax.rem(z + step, z_count)

        def rows_of(target):
            return pl.ds(pl.multiple_of(target * share, share), share)

        def c_copy(side, step):
            acc, landing, _, _ = sides[side]
            to_z = z_peer(step)
            return pltpu.make_async_remote_copy(
                src_ref=acc.at[:, rows_of(2 * to_z + 1 - core), :],
                dst_ref=landing.at[step],
                send_sem=c_send.at[side, step],
                recv_sem=c_recv.at[side, step],
                device_id=(blk, 2 * z + 1 - core),
                device_id_type=mesh_ids,
            )

        def z_copy(side, step):
            _, _, stage, landing = sides[side]
            return pltpu.make_async_remote_copy(
                src_ref=stage.at[step],
                dst_ref=landing.at[step],
                send_sem=z_send.at[side, step],
                recv_sem=z_recv.at[side, step],
                device_id=(blk, 2 * z_peer(step) + core),
                device_id_type=mesh_ids,
            )

        order = list(range(1, z_count)) + [0]
        for side in range(2):
            for step in order:
                c_copy(side, step).start()
        for side in range(2):
            acc, landing, stage, _ = sides[side]
            for step in order[:-1]:
                c_copy(side, step).wait_recv()
                both = acc[:, rows_of(2 * z_peer(step) + core), :] + landing[step]
                stage[step] = both.reshape(-1, both.shape[-1]).astype(bf)
                z_copy(side, step).start()

        def finish(side):
            acc, landing, _, terms = sides[side]
            c_copy(side, 0).wait_recv()
            total = acc[:, rows_of(seg), :] + landing[0]
            for step in range(1, z_count):
                z_copy(side, step).wait_recv()
                total = total + terms[step].astype(jnp.float32).reshape(total.shape)
            return total

        def o_copy(step):
            return pltpu.make_async_remote_copy(
                src_ref=done,
                dst_ref=others_ref.at[blk],
                send_sem=o_send.at[step],
                recv_sem=o_recv.at[step],
                device_id=(blk_peer(step), seg),
                device_id_type=mesh_ids,
            )

        keep = pltpu.make_async_copy(done, others_ref.at[blk], own_sem)
        done[...] = finish(0)
        for step in range(1, blk_count):
            o_copy(step).start()
        keep.start()
        total = finish(1)
        own = lag_order(
            [total[a, :, c * chan : (c + 1) * chan] for a in range(COARSE) for c in range(2 * FINE)]
        ) * scaling
        keep.wait()
        for step in range(1, blk_count):
            o_copy(step).wait()
        theirs = others_ref[came_from]
        got = lag_order(
            [theirs[c, :, a * chan : (a + 1) * chan] for a in range(COARSE) for c in reversed(range(2 * FINE))]
        ) * scaling
        out_ref[0] = jnp.where(parity == 0, own, got)
        out_ref[1] = jnp.where(parity == 0, got, own)
        for side in range(2):
            for step in order:
                c_copy(side, step).wait_send()
            for step in order[:-1]:
                z_copy(side, step).wait_send()
    else:
        plus_out[...] = plus[...]
        minus_out[...] = minus[...]
        picks_out[0] = came_from
        picks_out[1] = parity

    @pl.loop(0, chunks)
    def _(k):
        for step in range(1, seg_count):
            a_copy(k, step).wait_send()
        for step in range(1, blk_count):
            b_copy(k, step).wait_send()


def correlate(rows, pairing, fibre_lists, bound, tail, scaling):
    held, frequencies = rows.shape[1], rows.shape[2]
    chan = fibre_lists.shape[1]
    blk_count, seg_count = lax.axis_size("blk"), lax.axis_size("seg")
    chunks = frequencies // CHUNK
    cos, sin = phase_tables(frequencies)

    def by_chunk(table):
        return np.ascontiguousarray(table.reshape(-1, chunks, CHUNK).transpose(1, 0, 2))

    slots = np.arange(seg_count * held)
    number = slots // 2
    part = slots % 2
    across = np.broadcast_to(number[:, None], (slots.size, slots.size))
    places = np.concatenate([number[None], part[None], across]).astype(np.int32)

    wide = COARSE * chan
    f32, bf = jnp.float32, jnp.bfloat16
    share = chan // seg_count
    z_count = seg_count // 2
    plus_shape, minus_shape = (COARSE, chan, 2 * wide), (2 * FINE, chan, wide)
    p_shape, m_shape = (COARSE, share, 2 * wide), (2 * FINE, share, wide)
    dma = pltpu.SemaphoreType.DMA
    in_vmem, anywhere = pl.BlockSpec(memory_space=pltpu.VMEM), pl.BlockSpec(memory_space=pl.ANY)
    in_smem, picked = pl.BlockSpec(memory_space=pltpu.SMEM), jax.ShapeDtypeStruct((2,), jnp.int32)
    scratch = [
        pltpu.VMEM((blk_count * 2 * bound, seg_count * held), bf),
        pltpu.VMEM((4 * chan, blk_count * 2 * bound), bf),
        pltpu.VMEM((chunks, seg_count * held, CHUNK), bf),
        pltpu.VMEM((chunks, blk_count, 2 * bound, CHUNK), bf),
        pltpu.VMEM((chunks, blk_count, 2 * bound, CHUNK), bf),
        pltpu.VMEM((wide, 2 * CHUNK), bf),
        pltpu.VMEM((wide, 2 * CHUNK), bf),
        pltpu.VMEM((2 * wide, 2 * CHUNK), bf),
        pltpu.VMEM(plus_shape, f32),
        pltpu.VMEM(minus_shape, f32),
        dma((chunks, seg_count)),
        dma((chunks, seg_count)),
        dma((chunks, blk_count)),
        dma((chunks, blk_count)),
        dma((chunks,)),
    ]
    if tail:
        out_shape = [jax.ShapeDtypeStruct((2, share, chan, LH), f32)]
        out_specs = [in_vmem]
        flat_p, flat_m = (COARSE * share, 2 * wide), (2 * FINE * share, wide)
        scratch += [
            pltpu.VMEM((z_count,) + m_shape, f32),
            pltpu.VMEM((z_count,) + p_shape, f32),
            pltpu.VMEM((z_count,) + flat_m, bf),
            pltpu.VMEM((z_count,) + flat_p, bf),
            pltpu.VMEM((z_count,) + flat_m, bf),
            pltpu.VMEM((z_count,) + flat_p, bf),
            pltpu.VMEM(m_shape, f32),
            pltpu.VMEM((blk_count,) + m_shape, f32),
            dma((2, z_count)),
            dma((2, z_count)),
            dma((2, z_count)),
            dma((2, z_count)),
            dma((blk_count,)),
            dma((blk_count,)),
            dma(()),
        ]
    else:
        out_shape = [jax.ShapeDtypeStruct(plus_shape, f32), jax.ShapeDtypeStruct(minus_shape, f32), picked]
        out_specs = [in_vmem, in_vmem, in_smem]
    return pl.pallas_call(
        functools.partial(fused_kernel, chan, bound, tail, scaling),
        in_specs=[anywhere, in_smem] + [in_vmem] * 4,
        out_specs=out_specs,
        out_shape=out_shape,
        scratch_shapes=scratch,
        compiler_params=pltpu.CompilerParams(
            collective_id=0, has_side_effects=True, vmem_limit_bytes=56 * 1024 * 1024
        ),
        cost_estimate=pl.CostEstimate(
            flops=8 * wide * wide * frequencies * 2, bytes_accessed=16 * wide * wide, transcendentals=0
        ),
    )(rows, pairing, fibre_lists, places, by_chunk(cos), by_chunk(sin))


def local(spectra, fibre_lists, pairing):
    seg_all, held, _, frequencies = spectra.shape
    blk_count, seg_count = lax.axis_size("blk"), lax.axis_size("seg")
    chan = fibre_lists.shape[1]
    bound = 2 * (3 * chan // (2 * blk_count))

    rows = spectra.reshape(seg_all, 2 * held, frequencies)
    share = chan // seg_count
    tail = share % 8 == 0
    scaling = 1.0 / math.sqrt(frequencies * seg_all)
    results = correlate(rows, pairing, fibre_lists, bound, tail, scaling)
    if tail:
        return results[0][None]
    plus, minus, chosen = results
    plus = lax.psum_scatter(plus, "seg", scatter_dimension=1, tiled=True)
    minus = lax.psum_scatter(minus, "seg", scatter_dimension=1, tiled=True)
    others = lax.all_gather(minus, "blk", axis=0)
    other = lax.dynamic_index_in_dim(others, chosen[0], 0, keepdims=False)
    own = plus.reshape(COARSE, share, 2 * FINE, chan)
    own = jnp.transpose(own, (1, 3, 0, 2)).reshape(share, chan, LH) * scaling
    got = other.reshape(2 * FINE, share, COARSE, chan)[::-1]
    got = jnp.transpose(got, (1, 3, 2, 0)).reshape(share, chan, LH) * scaling
    first = chosen[1] == 0
    return jnp.stack([jnp.where(first, own, got), jnp.where(first, got, own)])[None]


def solution(mesh):
    in_specs = (P(None, ("blk", "seg"), None, None), P(), P())
    out_specs = P(None, "blk", "seg", None, None)
    return jax.shard_map(local, mesh=mesh, in_specs=in_specs, out_specs=out_specs, check_vma=False)
```

```python
import functools
import math

import numpy as np
import jax
import jax.numpy as jnp
from jax import lax
from jax.experimental import pallas as pl
from jax.experimental.pallas import tpu as pltpu
from jax.sharding import PartitionSpec as P

LH = 128
STEP = 16
COARSE = LH // STEP
FINE = STEP // 2
CHUNK = 512
AHEAD = 3
NT = (((1,), (1,)), ((), ()))


def phase_tables(frequencies):
    freq = np.arange(frequencies, dtype=np.float64)[None, :]
    coarse = (STEP * np.arange(COARSE, dtype=np.float64) + (STEP - 1) / 2)[:, None]
    fine = (np.arange(FINE, dtype=np.float64) + 0.5)[:, None]
    angles = np.concatenate([coarse, fine], 0) * freq * (math.pi / frequencies)
    return np.cos(angles).astype(np.float32), np.sin(angles).astype(np.float32)


def plan(chan, bound, width, blk, blk_count, pairing, lists, places, pack, unpack):
    count = lists.shape[0]
    lists_t = jnp.swapaxes(lists[...], 0, 1)
    i32, f32, bf = jnp.int32, jnp.float32, jnp.bfloat16

    def lowest(block):
        least = block
        at = block
        for _ in range(count // 2 - 1):
            at = pairing[0, at] ^ 1
            least = jnp.minimum(least, at)
        return least

    least = [lowest(jnp.int32(b)) for b in range(count)]
    owner = [
        jnp.where(least[b] < least[b ^ 1], jnp.int32(b), pairing[0, b]) // 2 for b in range(count)
    ]
    lead = jnp.int32(0)
    came_from = jnp.int32(0)
    for k in range(blk_count):
        first = least[2 * k] < least[2 * k + 1]
        lead = jnp.where(blk == k, jnp.where(first, 2 * k, 2 * k + 1), lead)
        came_from = jnp.where(blk == k, jnp.where(first, owner[2 * k + 1], owner[2 * k]), came_from)
    follow = pairing[0, lead]

    columns = places.shape[1]
    number = places[0:1, :]
    pair_of = jnp.zeros((1, columns), i32)
    for b in range(count):
        hit = lists_t[:, b : b + 1] == number + blk * width
        pair_of = pair_of + jnp.sum(jnp.where(hit, owner[b], 0), axis=0, keepdims=True)
    kinds = max(8, blk_count)
    real = (lax.broadcasted_iota(i32, (kinds, columns), 0) == pair_of) & (places[1:2, :] == 0)
    before = places[2 : 2 + columns, :] < number
    ranks = jnp.dot(
        jnp.where(real, 1.0, 0.0).astype(bf),
        jnp.where(before, 1.0, 0.0).astype(bf),
        preferred_element_type=f32,
    )
    mine = lax.broadcasted_iota(i32, (kinds, columns), 0) == pair_of
    rank = jnp.sum(jnp.where(mine, ranks, 0.0), axis=0, keepdims=True).astype(i32)
    target = pair_of * (2 * bound) + places[1:2, :] * bound + rank
    pack[...] = jnp.where(lax.broadcasted_iota(i32, pack.shape, 0) == target, 1.0, 0.0).astype(bf)

    roles = (lead, follow)
    zero_col, zero_row = jnp.zeros((chan, 1), i32), jnp.zeros((1, chan), i32)
    tall = [sum((jnp.where(role == b, lists_t[:, b : b + 1], 0) for b in range(count)), zero_col) for role in roles]
    flat = [sum((jnp.where(role == b, lists[b : b + 1, :], 0) for b in range(count)), zero_row) for role in roles]
    shift = width.bit_length() - 1
    lane = lax.broadcasted_iota(i32, (chan, unpack.shape[1]), 1)
    for r in range(2):
        rank = zero_col
        for other in flat:
            ahead = ((tall[r] >> shift) == (other >> shift)) & (other < tall[r])
            rank = rank + jnp.sum(jnp.where(ahead, 1, 0), axis=1, keepdims=True)
        spot = (tall[r] >> shift) * (2 * bound) + rank
        for part in range(2):
            hit = lane == spot + part * bound
            unpack[(2 * part + r) * chan : (2 * part + r + 1) * chan, :] = jnp.where(hit, 1.0, 0.0).astype(bf)
    return came_from, lead & 1


def lag_order(blocks):
    return jnp.swapaxes(jnp.swapaxes(jnp.stack(blocks), 0, 1), 1, 2)


def fused_kernel(
    chan, bound, tail, scaling, rows_ref, pairing, lists, places, cos_ref, sin_ref, *rest
):
    if tail:
        out_ref, *rest = rest
    else:
        plus_out, minus_out, picks_out, *rest = rest
    pack, unpack, col, packed, arr, xp, xm, yp, plus, minus, a_send, a_recv, b_send, b_recv, local_sem, *rest = rest
    blk_count, seg_count = lax.axis_size("blk"), lax.axis_size("seg")
    blk, seg = lax.axis_index("blk"), lax.axis_index("seg")
    chunks = col.shape[0]
    held = rows_ref.shape[1]
    width = col.shape[2]
    bf = jnp.bfloat16
    mesh_ids = pl.DeviceIdType.MESH

    def seg_peer(step):
        return lax.rem(seg + step, seg_count)

    def blk_peer(step):
        return lax.rem(blk + step, blk_count)

    barrier = pltpu.get_barrier_semaphore()
    for step in range(1, seg_count):
        pl.semaphore_signal(barrier, inc=1, device_id=(blk, seg_peer(step)), device_id_type=mesh_ids)
    for step in range(1, blk_count):
        pl.semaphore_signal(barrier, inc=1, device_id=(blk_peer(step), seg), device_id_type=mesh_ids)
    pl.semaphore_wait(barrier, seg_count + blk_count - 2)

    def a_copy(k, step):
        to = seg_peer(step)
        return pltpu.make_async_remote_copy(
            src_ref=rows_ref.at[to, :, pl.ds(pl.multiple_of(k * width, width), width)],
            dst_ref=col.at[k, pl.ds(pl.multiple_of(seg * held, held), held), :],
            send_sem=a_send.at[k, step],
            recv_sem=a_recv.at[k, step],
            device_id=(blk, to),
            device_id_type=mesh_ids,
        )

    def a_own(k):
        return pltpu.make_async_copy(
            rows_ref.at[seg, :, pl.ds(pl.multiple_of(k * width, width), width)],
            col.at[k, pl.ds(pl.multiple_of(seg * held, held), held), :],
            local_sem.at[k],
        )

    def b_copy(k, step):
        to = blk_peer(step)
        return pltpu.make_async_remote_copy(
            src_ref=packed.at[k, to],
            dst_ref=arr.at[k, blk],
            send_sem=b_send.at[k, step],
            recv_sem=b_recv.at[k, step],
            device_id=(to, seg),
            device_id_type=mesh_ids,
        )

    def b_own(k):
        return pltpu.make_async_copy(packed.at[k, blk], arr.at[k, blk], b_send.at[k, 0])

    def launch(k):
        for step in range(1, seg_count):
            a_copy(k, step).start()
        a_own(k).start()

    ahead = min(AHEAD, chunks)
    pl.loop(0, ahead)(launch)

    plus[...] = jnp.zeros_like(plus)
    minus[...] = jnp.zeros_like(minus)
    came_from, parity = plan(chan, bound, seg_count * held // 2, blk, blk_count, pairing, lists, places, pack, unpack)

    def route(k):
        for step in range(1, seg_count):
            a_copy(k, step).wait_recv()
        a_own(k).wait()
        mixed = jnp.dot(pack[...], col[k], preferred_element_type=jnp.float32).astype(bf)
        packed[k] = mixed.reshape(blk_count, 2 * bound, width)
        for step in range(1, blk_count):
            b_copy(k, step).start()
        b_own(k).start()

    def work(k):
        for step in range(1, blk_count):
            b_copy(k, step).wait_recv()
        b_own(k).wait()
        block = arr[k].reshape(blk_count * 2 * bound, width)
        rows = jnp.dot(unpack[...], block, preferred_element_type=jnp.float32)
        xr, yr = rows[0:chan], rows[chan : 2 * chan]
        xi, yi = rows[2 * chan : 3 * chan], rows[3 * chan : 4 * chan]
        re, im = pl.ds(0, width), pl.ds(width, width)
        for a in range(COARSE):
            c, s = cos_ref[k, a : a + 1, :], sin_ref[k, a : a + 1, :]
            rc, rs, ic, i_s = xr * c, xr * s, xi * c, xi * s
            at = pl.ds(a * chan, chan)
            xp[at, re] = (rc - i_s).astype(bf)
            xp[at, im] = (ic + rs).astype(bf)
            xm[at, re] = (rc + i_s).astype(bf)
            xm[at, im] = (ic - rs).astype(bf)
        for m in range(COARSE, COARSE + FINE):
            c, s = cos_ref[k, m : m + 1, :], sin_ref[k, m : m + 1, :]
            rc, rs, ic, i_s = yr * c, yr * s, yi * c, yi * s
            at, back = pl.ds((FINE + m - COARSE) * chan, chan), pl.ds((FINE - 1 - m + COARSE) * chan, chan)
            yp[at, re] = (rc + i_s).astype(bf)
            yp[at, im] = (ic - rs).astype(bf)
            yp[back, re] = (rc - i_s).astype(bf)
            yp[back, im] = (ic + rs).astype(bf)
        tile = 4 * chan

        @pl.loop(0, xm.shape[0] // tile)
        def _(t):
            at = pl.ds(pl.multiple_of(t * tile, tile), tile)
            term = lax.dot_general(yp[...], xm[at, :], NT, preferred_element_type=jnp.float32)
            minus[:, :, at] += term.reshape(2 * FINE, chan, tile)

        @pl.loop(0, yp.shape[0] // tile)
        def _(t):
            at = pl.ds(pl.multiple_of(t * tile, tile), tile)
            term = lax.dot_general(xp[...], yp[at, :], NT, preferred_element_type=jnp.float32)
            plus[:, :, at] += term.reshape(COARSE, chan, tile)

    def a_sent(k):
        for step in range(1, seg_count):
            a_copy(k, step).wait_send()

    route(0)

    @pl.loop(1, chunks)
    def _(k):
        @pl.when(k + ahead - 1 < chunks)
        def _():
            a_sent(k - 1)
            launch(k + ahead - 1)

        route(k)
        work(k - 1)

    work(chunks - 1)

    if tail:
        from_core_m, from_core_p, stage_m, stage_p, from_z_m, from_z_p, done, others_ref, c_send, c_recv, z_send, z_recv, o_send, o_recv, own_sem = rest
        share = chan // seg_count
        z_count = seg_count // 2
        core, z = lax.rem(seg, 2), lax.div(seg, 2)
        sides = ((minus, from_core_m, stage_m, from_z_m), (plus, from_core_p, stage_p, from_z_p))

        def z_peer(step):
            return lax.rem(z + step, z_count)

        def rows_of(target):
            return pl.ds(pl.multiple_of(target * share, share), share)

        def c_copy(side, step):
            acc, landing, _, _ = sides[side]
            to_z = z_peer(step)
            return pltpu.make_async_remote_copy(
                src_ref=acc.at[:, rows_of(2 * to_z + 1 - core), :],
                dst_ref=landing.at[step],
                send_sem=c_send.at[side, step],
                recv_sem=c_recv.at[side, step],
                device_id=(blk, 2 * z + 1 - core),
                device_id_type=mesh_ids,
            )

        def z_copy(side, step):
            _, _, stage, landing = sides[side]
            return pltpu.make_async_remote_copy(
                src_ref=stage.at[step],
                dst_ref=landing.at[step],
                send_sem=z_send.at[side, step],
                recv_sem=z_recv.at[side, step],
                device_id=(blk, 2 * z_peer(step) + core),
                device_id_type=mesh_ids,
            )

        order = list(range(1, z_count)) + [0]
        for side in range(2):
            for step in order:
                c_copy(side, step).start()
        for side in range(2):
            acc, landing, stage, _ = sides[side]
            for step in order[:-1]:
                c_copy(side, step).wait_recv()
                both = acc[:, rows_of(2 * z_peer(step) + core), :] + landing[step]
                stage[step] = both.reshape(-1, both.shape[-1]).astype(bf)
                z_copy(side, step).start()

        def finish(side):
            acc, landing, _, terms = sides[side]
            c_copy(side, 0).wait_recv()
            total = acc[:, rows_of(seg), :] + landing[0]
            for step in range(1, z_count):
                z_copy(side, step).wait_recv()
                total = total + terms[step].astype(jnp.float32).reshape(total.shape)
            return total

        def o_copy(step):
            return pltpu.make_async_remote_copy(
                src_ref=done,
                dst_ref=others_ref.at[blk],
                send_sem=o_send.at[step],
                recv_sem=o_recv.at[step],
                device_id=(blk_peer(step), seg),
                device_id_type=mesh_ids,
            )

        keep = pltpu.make_async_copy(done, others_ref.at[blk], own_sem)
        done[...] = finish(0)
        for step in range(1, blk_count):
            o_copy(step).start()
        keep.start()
        keep.wait()
        for step in range(1, blk_count):
            o_copy(step).wait()
        theirs = others_ref[came_from]
        got = lag_order(
            [theirs[c, :, a * chan : (a + 1) * chan] for a in range(COARSE) for c in reversed(range(2 * FINE))]
        ) * scaling
        out_ref[0] = got
        total = finish(1)
        own = lag_order(
            [total[a, :, c * chan : (c + 1) * chan] for a in range(COARSE) for c in range(2 * FINE)]
        ) * scaling
        got = out_ref[0]
        out_ref[0] = jnp.where(parity == 0, own, got)
        out_ref[1] = jnp.where(parity == 0, got, own)
        for side in range(2):
            for step in order:
                c_copy(side, step).wait_send()
            for step in order[:-1]:
                z_copy(side, step).wait_send()
    else:
        plus_out[...] = plus[...]
        minus_out[...] = minus[...]
        picks_out[0] = came_from
        picks_out[1] = parity

    pl.loop(chunks - ahead, chunks)(a_sent)

    @pl.loop(0, chunks)
    def _(k):
        for step in range(1, blk_count):
            b_copy(k, step).wait_send()


def correlate(rows, pairing, fibre_lists, bound, tail, scaling):
    held, frequencies = rows.shape[1], rows.shape[2]
    chan = fibre_lists.shape[1]
    blk_count, seg_count = lax.axis_size("blk"), lax.axis_size("seg")
    chunks = frequencies // CHUNK
    cos, sin = phase_tables(frequencies)

    def by_chunk(table):
        return np.ascontiguousarray(table.reshape(-1, chunks, CHUNK).transpose(1, 0, 2))

    slots = np.arange(seg_count * held)
    number = slots // 2
    part = slots % 2
    across = np.broadcast_to(number[:, None], (slots.size, slots.size))
    places = np.concatenate([number[None], part[None], across]).astype(np.int32)

    wide = COARSE * chan
    f32, bf = jnp.float32, jnp.bfloat16
    share = chan // seg_count
    z_count = seg_count // 2
    plus_shape, minus_shape = (COARSE, chan, 2 * wide), (2 * FINE, chan, wide)
    p_shape, m_shape = (COARSE, share, 2 * wide), (2 * FINE, share, wide)
    dma = pltpu.SemaphoreType.DMA
    in_vmem, anywhere = pl.BlockSpec(memory_space=pltpu.VMEM), pl.BlockSpec(memory_space=pl.ANY)
    in_smem, picked = pl.BlockSpec(memory_space=pltpu.SMEM), jax.ShapeDtypeStruct((2,), jnp.int32)
    scratch = [
        pltpu.VMEM((blk_count * 2 * bound, seg_count * held), bf),
        pltpu.VMEM((4 * chan, blk_count * 2 * bound), bf),
        pltpu.VMEM((chunks, seg_count * held, CHUNK), bf),
        pltpu.VMEM((chunks, blk_count, 2 * bound, CHUNK), bf),
        pltpu.VMEM((chunks, blk_count, 2 * bound, CHUNK), bf),
        pltpu.VMEM((wide, 2 * CHUNK), bf),
        pltpu.VMEM((wide, 2 * CHUNK), bf),
        pltpu.VMEM((2 * wide, 2 * CHUNK), bf),
        pltpu.VMEM(plus_shape, f32),
        pltpu.VMEM(minus_shape, f32),
        dma((chunks, seg_count)),
        dma((chunks, seg_count)),
        dma((chunks, blk_count)),
        dma((chunks, blk_count)),
        dma((chunks,)),
    ]
    if tail:
        out_shape = [jax.ShapeDtypeStruct((2, share, chan, LH), f32)]
        out_specs = [in_vmem]
        flat_p, flat_m = (COARSE * share, 2 * wide), (2 * FINE * share, wide)
        scratch += [
            pltpu.VMEM((z_count,) + m_shape, f32),
            pltpu.VMEM((z_count,) + p_shape, f32),
            pltpu.VMEM((z_count,) + flat_m, bf),
            pltpu.VMEM((z_count,) + flat_p, bf),
            pltpu.VMEM((z_count,) + flat_m, bf),
            pltpu.VMEM((z_count,) + flat_p, bf),
            pltpu.VMEM(m_shape, f32),
            pltpu.VMEM((blk_count,) + m_shape, f32),
            dma((2, z_count)),
            dma((2, z_count)),
            dma((2, z_count)),
            dma((2, z_count)),
            dma((blk_count,)),
            dma((blk_count,)),
            dma(()),
        ]
    else:
        out_shape = [jax.ShapeDtypeStruct(plus_shape, f32), jax.ShapeDtypeStruct(minus_shape, f32), picked]
        out_specs = [in_vmem, in_vmem, in_smem]
    return pl.pallas_call(
        functools.partial(fused_kernel, chan, bound, tail, scaling),
        in_specs=[anywhere, in_smem] + [in_vmem] * 4,
        out_specs=out_specs,
        out_shape=out_shape,
        scratch_shapes=scratch,
        compiler_params=pltpu.CompilerParams(
            collective_id=0, has_side_effects=True, vmem_limit_bytes=56 * 1024 * 1024
        ),
        cost_estimate=pl.CostEstimate(
            flops=8 * wide * wide * frequencies * 2, bytes_accessed=16 * wide * wide, transcendentals=0
        ),
    )(rows, pairing, fibre_lists, places, by_chunk(cos), by_chunk(sin))


def local(spectra, fibre_lists, pairing):
    seg_all, held, _, frequencies = spectra.shape
    blk_count, seg_count = lax.axis_size("blk"), lax.axis_size("seg")
    chan = fibre_lists.shape[1]
    bound = 2 * (3 * chan // (2 * blk_count))

    rows = spectra.reshape(seg_all, 2 * held, frequencies)
    share = chan // seg_count
    tail = share % 8 == 0
    scaling = 1.0 / math.sqrt(frequencies * seg_all)
    results = correlate(rows, pairing, fibre_lists, bound, tail, scaling)
    if tail:
        return results[0][None]
    plus, minus, chosen = results
    plus = lax.psum_scatter(plus, "seg", scatter_dimension=1, tiled=True)
    minus = lax.psum_scatter(minus, "seg", scatter_dimension=1, tiled=True)
    others = lax.all_gather(minus, "blk", axis=0)
    other = lax.dynamic_index_in_dim(others, chosen[0], 0, keepdims=False)
    own = plus.reshape(COARSE, share, 2 * FINE, chan)
    own = jnp.transpose(own, (1, 3, 0, 2)).reshape(share, chan, LH) * scaling
    got = other.reshape(2 * FINE, share, COARSE, chan)[::-1]
    got = jnp.transpose(got, (1, 3, 2, 0)).reshape(share, chan, LH) * scaling
    first = chosen[1] == 0
    return jnp.stack([jnp.where(first, own, got), jnp.where(first, got, own)])[None]


def solution(mesh):
    in_specs = (P(None, ("blk", "seg"), None, None), P(), P())
    out_specs = P(None, "blk", "seg", None, None)
    return jax.shard_map(local, mesh=mesh, in_specs=in_specs, out_specs=out_specs, check_vma=False)
```

```python
import functools
import math

import numpy as np
import jax
import jax.numpy as jnp
from jax import lax
from jax.experimental import pallas as pl
from jax.experimental.pallas import tpu as pltpu
from jax.sharding import PartitionSpec as P

LH = 128
STEP = 16
COARSE = LH // STEP
FINE = STEP // 2
CHUNK = 512
AHEAD = 3
NT = (((1,), (1,)), ((), ()))


def phase_tables(frequencies):
    freq = np.arange(frequencies, dtype=np.float64)[None, :]
    coarse = (STEP * np.arange(COARSE, dtype=np.float64) + (STEP - 1) / 2)[:, None]
    fine = (np.arange(FINE, dtype=np.float64) + 0.5)[:, None]
    angles = np.concatenate([coarse, fine], 0) * freq * (math.pi / frequencies)
    return np.cos(angles).astype(np.float32), np.sin(angles).astype(np.float32)


def plan(chan, bound, width, blk, blk_count, pairing, lists, places, pack, unpack):
    count = lists.shape[0]
    lists_t = jnp.swapaxes(lists[...], 0, 1)
    i32, f32, bf = jnp.int32, jnp.float32, jnp.bfloat16

    def lowest(block):
        least = block
        at = block
        for _ in range(count // 2 - 1):
            at = pairing[0, at] ^ 1
            least = jnp.minimum(least, at)
        return least

    least = [lowest(jnp.int32(b)) for b in range(count)]
    owner = [
        jnp.where(least[b] < least[b ^ 1], jnp.int32(b), pairing[0, b]) // 2 for b in range(count)
    ]
    lead = jnp.int32(0)
    came_from = jnp.int32(0)
    for k in range(blk_count):
        first = least[2 * k] < least[2 * k + 1]
        lead = jnp.where(blk == k, jnp.where(first, 2 * k, 2 * k + 1), lead)
        came_from = jnp.where(blk == k, jnp.where(first, owner[2 * k + 1], owner[2 * k]), came_from)
    follow = pairing[0, lead]

    columns = places.shape[1]
    number = places[0:1, :]
    pair_of = jnp.zeros((1, columns), i32)
    for b in range(count):
        hit = lists_t[:, b : b + 1] == number + blk * width
        pair_of = pair_of + jnp.sum(jnp.where(hit, owner[b], 0), axis=0, keepdims=True)
    kinds = max(8, blk_count)
    real = (lax.broadcasted_iota(i32, (kinds, columns), 0) == pair_of) & (places[1:2, :] == 0)
    before = places[2 : 2 + columns, :] < number
    ranks = jnp.dot(
        jnp.where(real, 1.0, 0.0).astype(bf),
        jnp.where(before, 1.0, 0.0).astype(bf),
        preferred_element_type=f32,
    )
    mine = lax.broadcasted_iota(i32, (kinds, columns), 0) == pair_of
    rank = jnp.sum(jnp.where(mine, ranks, 0.0), axis=0, keepdims=True).astype(i32)
    target = pair_of * (2 * bound) + places[1:2, :] * bound + rank
    pack[...] = jnp.where(lax.broadcasted_iota(i32, pack.shape, 0) == target, 1.0, 0.0).astype(bf)

    roles = (lead, follow)
    zero_col, zero_row = jnp.zeros((chan, 1), i32), jnp.zeros((1, chan), i32)
    tall = [sum((jnp.where(role == b, lists_t[:, b : b + 1], 0) for b in range(count)), zero_col) for role in roles]
    flat = [sum((jnp.where(role == b, lists[b : b + 1, :], 0) for b in range(count)), zero_row) for role in roles]
    shift = width.bit_length() - 1
    lane = lax.broadcasted_iota(i32, (chan, unpack.shape[1]), 1)
    for r in range(2):
        rank = zero_col
        for other in flat:
            ahead = ((tall[r] >> shift) == (other >> shift)) & (other < tall[r])
            rank = rank + jnp.sum(jnp.where(ahead, 1, 0), axis=1, keepdims=True)
        spot = (tall[r] >> shift) * (2 * bound) + rank
        for part in range(2):
            hit = lane == spot + part * bound
            unpack[(2 * part + r) * chan : (2 * part + r + 1) * chan, :] = jnp.where(hit, 1.0, 0.0).astype(bf)
    return came_from, lead & 1


def lag_order(blocks):
    return jnp.swapaxes(jnp.swapaxes(jnp.stack(blocks), 0, 1), 1, 2)


def fused_kernel(
    chan, bound, tail, scaling, rows_ref, pairing, lists, places, cos_ref, sin_ref, *rest
):
    if tail:
        out_ref, *rest = rest
    else:
        plus_out, minus_out, picks_out, *rest = rest
    pack, unpack, col, packed, arr, xp, xm, yp, plus, minus, a_send, a_recv, b_send, b_recv, local_sem, *rest = rest
    blk_count, seg_count = lax.axis_size("blk"), lax.axis_size("seg")
    blk, seg = lax.axis_index("blk"), lax.axis_index("seg")
    chunks = col.shape[0]
    held = rows_ref.shape[1]
    width = col.shape[3]
    bf = jnp.bfloat16
    mesh_ids = pl.DeviceIdType.MESH

    def seg_peer(step):
        return lax.rem(seg + step, seg_count)

    def blk_peer(step):
        return lax.rem(blk + step, blk_count)

    barrier = pltpu.get_barrier_semaphore()
    for step in range(1, seg_count):
        pl.semaphore_signal(barrier, inc=1, device_id=(blk, seg_peer(step)), device_id_type=mesh_ids)
    for step in range(1, blk_count):
        pl.semaphore_signal(barrier, inc=1, device_id=(blk_peer(step), seg), device_id_type=mesh_ids)
    pl.semaphore_wait(barrier, seg_count + blk_count - 2)

    def a_copy(k, step):
        to = seg_peer(step)
        return pltpu.make_async_remote_copy(
            src_ref=rows_ref.at[to, :, :, pl.ds(pl.multiple_of(k * width, width), width)],
            dst_ref=col.at[k, pl.ds(pl.multiple_of(seg * held, held), held)],
            send_sem=a_send.at[k, step],
            recv_sem=a_recv.at[k, step],
            device_id=(blk, to),
            device_id_type=mesh_ids,
        )

    def a_own(k):
        return pltpu.make_async_copy(
            rows_ref.at[seg, :, :, pl.ds(pl.multiple_of(k * width, width), width)],
            col.at[k, pl.ds(pl.multiple_of(seg * held, held), held)],
            local_sem.at[k],
        )

    def b_copy(k, step):
        to = blk_peer(step)
        return pltpu.make_async_remote_copy(
            src_ref=packed.at[k, to],
            dst_ref=arr.at[k, blk],
            send_sem=b_send.at[k, step],
            recv_sem=b_recv.at[k, step],
            device_id=(to, seg),
            device_id_type=mesh_ids,
        )

    def b_own(k):
        return pltpu.make_async_copy(packed.at[k, blk], arr.at[k, blk], b_send.at[k, 0])

    def launch(k):
        for step in range(1, seg_count):
            a_copy(k, step).start()
        a_own(k).start()

    ahead = min(AHEAD, chunks)
    pl.loop(0, ahead)(launch)

    plus[...] = jnp.zeros_like(plus)
    minus[...] = jnp.zeros_like(minus)
    came_from, parity = plan(chan, bound, seg_count * held, blk, blk_count, pairing, lists, places, pack, unpack)

    def route(k):
        for step in range(1, seg_count):
            a_copy(k, step).wait_recv()
        a_own(k).wait()
        mixed = jnp.dot(pack[...], col[k].reshape(2 * seg_count * held, width), preferred_element_type=jnp.float32).astype(bf)
        packed[k] = mixed.reshape(blk_count, 2 * bound, width)
        for step in range(1, blk_count):
            b_copy(k, step).start()
        b_own(k).start()

    def work(k):
        for step in range(1, blk_count):
            b_copy(k, step).wait_recv()
        b_own(k).wait()
        block = arr[k].reshape(blk_count * 2 * bound, width)
        rows = jnp.dot(unpack[...], block, preferred_element_type=jnp.float32)
        xr, yr = rows[0:chan], rows[chan : 2 * chan]
        xi, yi = rows[2 * chan : 3 * chan], rows[3 * chan : 4 * chan]
        re, im = pl.ds(0, width), pl.ds(width, width)
        for a in range(COARSE):
            c, s = cos_ref[k, a : a + 1, :], sin_ref[k, a : a + 1, :]
            rc, rs, ic, i_s = xr * c, xr * s, xi * c, xi * s
            at = pl.ds(a * chan, chan)
            xp[at, re] = (rc - i_s).astype(bf)
            xp[at, im] = (ic + rs).astype(bf)
            xm[at, re] = (rc + i_s).astype(bf)
            xm[at, im] = (ic - rs).astype(bf)
        for m in range(COARSE, COARSE + FINE):
            c, s = cos_ref[k, m : m + 1, :], sin_ref[k, m : m + 1, :]
            rc, rs, ic, i_s = yr * c, yr * s, yi * c, yi * s
            at, back = pl.ds((FINE + m - COARSE) * chan, chan), pl.ds((FINE - 1 - m + COARSE) * chan, chan)
            yp[at, re] = (rc + i_s).astype(bf)
            yp[at, im] = (ic - rs).astype(bf)
            yp[back, re] = (rc - i_s).astype(bf)
            yp[back, im] = (ic + rs).astype(bf)
        tile = 4 * chan

        @pl.loop(0, xm.shape[0] // tile)
        def _(t):
            at = pl.ds(pl.multiple_of(t * tile, tile), tile)
            term = lax.dot_general(yp[...], xm[at, :], NT, preferred_element_type=jnp.float32)
            minus[:, :, at] += term.reshape(2 * FINE, chan, tile)

        @pl.loop(0, yp.shape[0] // tile)
        def _(t):
            at = pl.ds(pl.multiple_of(t * tile, tile), tile)
            term = lax.dot_general(xp[...], yp[at, :], NT, preferred_element_type=jnp.float32)
            plus[:, :, at] += term.reshape(COARSE, chan, tile)

    def a_sent(k):
        for step in range(1, seg_count):
            a_copy(k, step).wait_send()

    route(0)

    @pl.loop(1, chunks)
    def _(k):
        @pl.when(k + ahead - 1 < chunks)
        def _():
            a_sent(k - 1)
            launch(k + ahead - 1)

        route(k)
        work(k - 1)

    work(chunks - 1)

    if tail:
        from_core_m, from_core_p, stage_m, stage_p, from_z_m, from_z_p, done, others_ref, c_send, c_recv, z_send, z_recv, o_send, o_recv, own_sem = rest
        share = chan // seg_count
        z_count = seg_count // 2
        core, z = lax.rem(seg, 2), lax.div(seg, 2)
        sides = ((minus, from_core_m, stage_m, from_z_m), (plus, from_core_p, stage_p, from_z_p))

        def z_peer(step):
            return lax.rem(z + step, z_count)

        def rows_of(target):
            return pl.ds(pl.multiple_of(target * share, share), share)

        def c_copy(side, step):
            acc, landing, _, _ = sides[side]
            to_z = z_peer(step)
            return pltpu.make_async_remote_copy(
                src_ref=acc.at[:, rows_of(2 * to_z + 1 - core), :],
                dst_ref=landing.at[step],
                send_sem=c_send.at[side, step],
                recv_sem=c_recv.at[side, step],
                device_id=(blk, 2 * z + 1 - core),
                device_id_type=mesh_ids,
            )

        def z_copy(side, step):
            _, _, stage, landing = sides[side]
            return pltpu.make_async_remote_copy(
                src_ref=stage.at[step],
                dst_ref=landing.at[step],
                send_sem=z_send.at[side, step],
                recv_sem=z_recv.at[side, step],
                device_id=(blk, 2 * z_peer(step) + core),
                device_id_type=mesh_ids,
            )

        order = list(range(1, z_count)) + [0]
        for side in range(2):
            for step in order:
                c_copy(side, step).start()
        for side in range(2):
            acc, landing, stage, _ = sides[side]
            for step in order[:-1]:
                c_copy(side, step).wait_recv()
                both = acc[:, rows_of(2 * z_peer(step) + core), :] + landing[step]
                stage[step] = both.reshape(-1, both.shape[-1]).astype(bf)
                z_copy(side, step).start()

        def finish(side):
            acc, landing, _, terms = sides[side]
            c_copy(side, 0).wait_recv()
            total = acc[:, rows_of(seg), :] + landing[0]
            for step in range(1, z_count):
                z_copy(side, step).wait_recv()
                total = total + terms[step].astype(jnp.float32).reshape(total.shape)
            return total

        def o_copy(step):
            return pltpu.make_async_remote_copy(
                src_ref=done,
                dst_ref=others_ref.at[blk],
                send_sem=o_send.at[step],
                recv_sem=o_recv.at[step],
                device_id=(blk_peer(step), seg),
                device_id_type=mesh_ids,
            )

        keep = pltpu.make_async_copy(done, others_ref.at[blk], own_sem)
        done[...] = finish(0)
        for step in range(1, blk_count):
            o_copy(step).start()
        keep.start()
        keep.wait()
        for step in range(1, blk_count):
            o_copy(step).wait()
        theirs = others_ref[came_from]
        got = lag_order(
            [theirs[c, :, a * chan : (a + 1) * chan] for a in range(COARSE) for c in reversed(range(2 * FINE))]
        ) * scaling
        out_ref[0] = got
        total = finish(1)
        own = lag_order(
            [total[a, :, c * chan : (c + 1) * chan] for a in range(COARSE) for c in range(2 * FINE)]
        ) * scaling
        got = out_ref[0]
        out_ref[0] = jnp.where(parity == 0, own, got)
        out_ref[1] = jnp.where(parity == 0, got, own)
        for side in range(2):
            for step in order:
                c_copy(side, step).wait_send()
            for step in order[:-1]:
                z_copy(side, step).wait_send()
    else:
        plus_out[...] = plus[...]
        minus_out[...] = minus[...]
        picks_out[0] = came_from
        picks_out[1] = parity

    pl.loop(chunks - ahead, chunks)(a_sent)

    @pl.loop(0, chunks)
    def _(k):
        for step in range(1, blk_count):
            b_copy(k, step).wait_send()


def correlate(rows, pairing, fibre_lists, bound, tail, scaling):
    held, frequencies = rows.shape[1], rows.shape[3]
    chan = fibre_lists.shape[1]
    blk_count, seg_count = lax.axis_size("blk"), lax.axis_size("seg")
    chunks = frequencies // CHUNK
    cos, sin = phase_tables(frequencies)

    def by_chunk(table):
        return np.ascontiguousarray(table.reshape(-1, chunks, CHUNK).transpose(1, 0, 2))

    slots = np.arange(2 * seg_count * held)
    number = slots // 2
    part = slots % 2
    across = np.broadcast_to(number[:, None], (slots.size, slots.size))
    places = np.concatenate([number[None], part[None], across]).astype(np.int32)

    wide = COARSE * chan
    f32, bf = jnp.float32, jnp.bfloat16
    share = chan // seg_count
    z_count = seg_count // 2
    plus_shape, minus_shape = (COARSE, chan, 2 * wide), (2 * FINE, chan, wide)
    p_shape, m_shape = (COARSE, share, 2 * wide), (2 * FINE, share, wide)
    dma = pltpu.SemaphoreType.DMA
    in_vmem, anywhere = pl.BlockSpec(memory_space=pltpu.VMEM), pl.BlockSpec(memory_space=pl.ANY)
    in_smem, picked = pl.BlockSpec(memory_space=pltpu.SMEM), jax.ShapeDtypeStruct((2,), jnp.int32)
    scratch = [
        pltpu.VMEM((blk_count * 2 * bound, 2 * seg_count * held), bf),
        pltpu.VMEM((4 * chan, blk_count * 2 * bound), bf),
        pltpu.VMEM((chunks, seg_count * held, 2, CHUNK), bf),
        pltpu.VMEM((chunks, blk_count, 2 * bound, CHUNK), bf),
        pltpu.VMEM((chunks, blk_count, 2 * bound, CHUNK), bf),
        pltpu.VMEM((wide, 2 * CHUNK), bf),
        pltpu.VMEM((wide, 2 * CHUNK), bf),
        pltpu.VMEM((2 * wide, 2 * CHUNK), bf),
        pltpu.VMEM(plus_shape, f32),
        pltpu.VMEM(minus_shape, f32),
        dma((chunks, seg_count)),
        dma((chunks, seg_count)),
        dma((chunks, blk_count)),
        dma((chunks, blk_count)),
        dma((chunks,)),
    ]
    if tail:
        out_shape = [jax.ShapeDtypeStruct((2, share, chan, LH), f32)]
        out_specs = [in_vmem]
        flat_p, flat_m = (COARSE * share, 2 * wide), (2 * FINE * share, wide)
        scratch += [
            pltpu.VMEM((z_count,) + m_shape, f32),
            pltpu.VMEM((z_count,) + p_shape, f32),
            pltpu.VMEM((z_count,) + flat_m, bf),
            pltpu.VMEM((z_count,) + flat_p, bf),
            pltpu.VMEM((z_count,) + flat_m, bf),
            pltpu.VMEM((z_count,) + flat_p, bf),
            pltpu.VMEM(m_shape, f32),
            pltpu.VMEM((blk_count,) + m_shape, f32),
            dma((2, z_count)),
            dma((2, z_count)),
            dma((2, z_count)),
            dma((2, z_count)),
            dma((blk_count,)),
            dma((blk_count,)),
            dma(()),
        ]
    else:
        out_shape = [jax.ShapeDtypeStruct(plus_shape, f32), jax.ShapeDtypeStruct(minus_shape, f32), picked]
        out_specs = [in_vmem, in_vmem, in_smem]
    return pl.pallas_call(
        functools.partial(fused_kernel, chan, bound, tail, scaling),
        in_specs=[anywhere, in_smem] + [in_vmem] * 4,
        out_specs=out_specs,
        out_shape=out_shape,
        scratch_shapes=scratch,
        compiler_params=pltpu.CompilerParams(
            collective_id=0, has_side_effects=True, vmem_limit_bytes=56 * 1024 * 1024
        ),
        cost_estimate=pl.CostEstimate(
            flops=8 * wide * wide * frequencies * 2, bytes_accessed=16 * wide * wide, transcendentals=0
        ),
    )(rows, pairing, fibre_lists, places, by_chunk(cos), by_chunk(sin))


def local(spectra, fibre_lists, pairing):
    seg_all, frequencies = spectra.shape[0], spectra.shape[3]
    blk_count, seg_count = lax.axis_size("blk"), lax.axis_size("seg")
    chan = fibre_lists.shape[1]
    bound = 2 * (3 * chan // (2 * blk_count))

    share = chan // seg_count
    tail = share % 8 == 0
    scaling = 1.0 / math.sqrt(frequencies * seg_all)
    results = correlate(spectra, pairing, fibre_lists, bound, tail, scaling)
    if tail:
        return results[0][None]
    plus, minus, chosen = results
    plus = lax.psum_scatter(plus, "seg", scatter_dimension=1, tiled=True)
    minus = lax.psum_scatter(minus, "seg", scatter_dimension=1, tiled=True)
    others = lax.all_gather(minus, "blk", axis=0)
    other = lax.dynamic_index_in_dim(others, chosen[0], 0, keepdims=False)
    own = plus.reshape(COARSE, share, 2 * FINE, chan)
    own = jnp.transpose(own, (1, 3, 0, 2)).reshape(share, chan, LH) * scaling
    got = other.reshape(2 * FINE, share, COARSE, chan)[::-1]
    got = jnp.transpose(got, (1, 3, 2, 0)).reshape(share, chan, LH) * scaling
    first = chosen[1] == 0
    return jnp.stack([jnp.where(first, own, got), jnp.where(first, got, own)])[None]


def solution(mesh):
    in_specs = (P(None, ("blk", "seg"), None, None), P(), P())
    out_specs = P(None, "blk", "seg", None, None)
    return jax.shard_map(local, mesh=mesh, in_specs=in_specs, out_specs=out_specs, check_vma=False)
```

```python
import functools
import math

import numpy as np
import jax
import jax.numpy as jnp
from jax import lax
from jax.experimental import pallas as pl
from jax.experimental.pallas import tpu as pltpu
from jax.sharding import PartitionSpec as P

LH = 128
STEP = 16
COARSE = LH // STEP
FINE = STEP // 2
CHUNK = 512
AHEAD = 3
NT = (((1,), (1,)), ((), ()))


def phase_tables(frequencies):
    freq = np.arange(frequencies, dtype=np.float64)[None, :]
    coarse = (STEP * np.arange(COARSE, dtype=np.float64) + (STEP - 1) / 2)[:, None]
    fine = (np.arange(FINE, dtype=np.float64) + 0.5)[:, None]
    angles = np.concatenate([coarse, fine], 0) * freq * (math.pi / frequencies)
    return np.cos(angles).astype(np.float32), np.sin(angles).astype(np.float32)


def plan(chan, bound, width, blk, blk_count, pairing, lists, places, pack, unpack):
    count = lists.shape[0]
    lists_t = jnp.swapaxes(lists[...], 0, 1)
    i32, f32, bf = jnp.int32, jnp.float32, jnp.bfloat16

    def lowest(block):
        least = block
        at = block
        for _ in range(count // 2 - 1):
            at = pairing[0, at] ^ 1
            least = jnp.minimum(least, at)
        return least

    least = [lowest(jnp.int32(b)) for b in range(count)]
    owner = [
        jnp.where(least[b] < least[b ^ 1], jnp.int32(b), pairing[0, b]) // 2 for b in range(count)
    ]
    lead = jnp.int32(0)
    came_from = jnp.int32(0)
    for k in range(blk_count):
        first = least[2 * k] < least[2 * k + 1]
        lead = jnp.where(blk == k, jnp.where(first, 2 * k, 2 * k + 1), lead)
        came_from = jnp.where(blk == k, jnp.where(first, owner[2 * k + 1], owner[2 * k]), came_from)
    follow = pairing[0, lead]

    columns = places.shape[1]
    number = places[0:1, :]
    pair_of = jnp.zeros((1, columns), i32)
    for b in range(count):
        hit = lists_t[:, b : b + 1] == number + blk * width
        pair_of = pair_of + jnp.sum(jnp.where(hit, owner[b], 0), axis=0, keepdims=True)
    kinds = max(8, blk_count)
    real = (lax.broadcasted_iota(i32, (kinds, columns), 0) == pair_of) & (places[1:2, :] == 0)
    before = places[2 : 2 + columns, :] < number
    ranks = jnp.dot(
        jnp.where(real, 1.0, 0.0).astype(bf),
        jnp.where(before, 1.0, 0.0).astype(bf),
        preferred_element_type=f32,
    )
    mine = lax.broadcasted_iota(i32, (kinds, columns), 0) == pair_of
    rank = jnp.sum(jnp.where(mine, ranks, 0.0), axis=0, keepdims=True).astype(i32)
    target = pair_of * (2 * bound) + places[1:2, :] * bound + rank
    pack[...] = jnp.where(lax.broadcasted_iota(i32, pack.shape, 0) == target, 1.0, 0.0).astype(bf)

    roles = (lead, follow)
    zero_col, zero_row = jnp.zeros((chan, 1), i32), jnp.zeros((1, chan), i32)
    tall = [sum((jnp.where(role == b, lists_t[:, b : b + 1], 0) for b in range(count)), zero_col) for role in roles]
    flat = [sum((jnp.where(role == b, lists[b : b + 1, :], 0) for b in range(count)), zero_row) for role in roles]
    shift = width.bit_length() - 1
    lane = lax.broadcasted_iota(i32, (chan, unpack.shape[1]), 1)
    for r in range(2):
        rank = zero_col
        for other in flat:
            ahead = ((tall[r] >> shift) == (other >> shift)) & (other < tall[r])
            rank = rank + jnp.sum(jnp.where(ahead, 1, 0), axis=1, keepdims=True)
        spot = (tall[r] >> shift) * (2 * bound) + rank
        for part in range(2):
            hit = lane == spot + part * bound
            unpack[(2 * part + r) * chan : (2 * part + r + 1) * chan, :] = jnp.where(hit, 1.0, 0.0).astype(bf)
    return came_from, lead & 1


def lag_order(blocks):
    return jnp.swapaxes(jnp.swapaxes(jnp.stack(blocks), 0, 1), 1, 2)


def fused_kernel(
    chan, bound, tail, scaling, rows_ref, pairing, lists, places, cos_ref, sin_ref, *rest
):
    if tail:
        out_ref, *rest = rest
    else:
        plus_out, minus_out, picks_out, *rest = rest
    pack, unpack, col, packed, arr, xp, xm, yp, plus, minus, a_send, a_recv, b_send, b_recv, local_sem, *rest = rest
    blk_count, seg_count = lax.axis_size("blk"), lax.axis_size("seg")
    blk, seg = lax.axis_index("blk"), lax.axis_index("seg")
    chunks = col.shape[0]
    held = rows_ref.shape[1]
    width = col.shape[3]
    bf = jnp.bfloat16
    mesh_ids = pl.DeviceIdType.MESH

    def seg_peer(step):
        return lax.rem(seg + step, seg_count)

    def blk_peer(step):
        return lax.rem(blk + step, blk_count)

    barrier = pltpu.get_barrier_semaphore()
    for step in range(1, seg_count):
        pl.semaphore_signal(barrier, inc=1, device_id=(blk, seg_peer(step)), device_id_type=mesh_ids)
    for step in range(1, blk_count):
        pl.semaphore_signal(barrier, inc=1, device_id=(blk_peer(step), seg), device_id_type=mesh_ids)
    pl.semaphore_wait(barrier, seg_count + blk_count - 2)

    def a_copy(k, step):
        to = seg_peer(step)
        return pltpu.make_async_remote_copy(
            src_ref=rows_ref.at[to, :, :, pl.ds(pl.multiple_of(k * width, width), width)],
            dst_ref=col.at[k, pl.ds(pl.multiple_of(seg * held, held), held)],
            send_sem=a_send.at[k, step],
            recv_sem=a_recv.at[k, step],
            device_id=(blk, to),
            device_id_type=mesh_ids,
        )

    def a_own(k):
        return pltpu.make_async_copy(
            rows_ref.at[seg, :, :, pl.ds(pl.multiple_of(k * width, width), width)],
            col.at[k, pl.ds(pl.multiple_of(seg * held, held), held)],
            local_sem.at[k],
        )

    def b_copy(k, step):
        to = blk_peer(step)
        return pltpu.make_async_remote_copy(
            src_ref=packed.at[k, to],
            dst_ref=arr.at[k, blk],
            send_sem=b_send.at[k, step],
            recv_sem=b_recv.at[k, step],
            device_id=(to, seg),
            device_id_type=mesh_ids,
        )

    def b_own(k):
        return pltpu.make_async_copy(packed.at[k, blk], arr.at[k, blk], b_send.at[k, 0])

    def launch(k):
        for step in range(1, seg_count):
            a_copy(k, step).start()
        a_own(k).start()

    ahead = min(AHEAD, chunks)
    pl.loop(0, ahead)(launch)

    plus[...] = jnp.zeros_like(plus)
    minus[...] = jnp.zeros_like(minus)
    came_from, parity = plan(chan, bound, seg_count * held, blk, blk_count, pairing, lists, places, pack, unpack)

    def route(k):
        for step in range(1, seg_count):
            a_copy(k, step).wait_recv()
        a_own(k).wait()
        mixed = jnp.dot(pack[...], col[k].reshape(2 * seg_count * held, width), preferred_element_type=jnp.float32).astype(bf)
        packed[k] = mixed.reshape(blk_count, 2 * bound, width)
        for step in range(1, blk_count):
            b_copy(k, step).start()
        b_own(k).start()

    def work(k, minus_done=None):
        for step in range(1, blk_count):
            b_copy(k, step).wait_recv()
        b_own(k).wait()
        block = arr[k].reshape(blk_count * 2 * bound, width)
        rows = jnp.dot(unpack[...], block, preferred_element_type=jnp.float32)
        xr, yr = rows[0:chan], rows[chan : 2 * chan]
        xi, yi = rows[2 * chan : 3 * chan], rows[3 * chan : 4 * chan]
        re, im = pl.ds(0, width), pl.ds(width, width)
        for a in range(COARSE):
            c, s = cos_ref[k, a : a + 1, :], sin_ref[k, a : a + 1, :]
            rc, rs, ic, i_s = xr * c, xr * s, xi * c, xi * s
            at = pl.ds(a * chan, chan)
            xp[at, re] = (rc - i_s).astype(bf)
            xp[at, im] = (ic + rs).astype(bf)
            xm[at, re] = (rc + i_s).astype(bf)
            xm[at, im] = (ic - rs).astype(bf)
        for m in range(COARSE, COARSE + FINE):
            c, s = cos_ref[k, m : m + 1, :], sin_ref[k, m : m + 1, :]
            rc, rs, ic, i_s = yr * c, yr * s, yi * c, yi * s
            at, back = pl.ds((FINE + m - COARSE) * chan, chan), pl.ds((FINE - 1 - m + COARSE) * chan, chan)
            yp[at, re] = (rc + i_s).astype(bf)
            yp[at, im] = (ic - rs).astype(bf)
            yp[back, re] = (rc - i_s).astype(bf)
            yp[back, im] = (ic + rs).astype(bf)
        tile = 4 * chan

        @pl.loop(0, xm.shape[0] // tile)
        def _(t):
            at = pl.ds(pl.multiple_of(t * tile, tile), tile)
            term = lax.dot_general(yp[...], xm[at, :], NT, preferred_element_type=jnp.float32)
            minus[:, :, at] += term.reshape(2 * FINE, chan, tile)

        if minus_done:
            minus_done()

        @pl.loop(0, yp.shape[0] // tile)
        def _(t):
            at = pl.ds(pl.multiple_of(t * tile, tile), tile)
            term = lax.dot_general(xp[...], yp[at, :], NT, preferred_element_type=jnp.float32)
            plus[:, :, at] += term.reshape(COARSE, chan, tile)

    def a_sent(k):
        for step in range(1, seg_count):
            a_copy(k, step).wait_send()

    route(0)

    @pl.loop(1, chunks)
    def _(k):
        @pl.when(k + ahead - 1 < chunks)
        def _():
            a_sent(k - 1)
            launch(k + ahead - 1)

        route(k)
        work(k - 1)

    if tail:
        from_core_m, from_core_p, stage_m, stage_p, from_z_m, from_z_p, done, done_p, others_ref, c_send, c_recv, z_send, z_recv, o_send, o_recv, own_sem = rest
        share = chan // seg_count
        z_count = seg_count // 2
        core, z = lax.rem(seg, 2), lax.div(seg, 2)
        sides = ((minus, from_core_m, stage_m, from_z_m), (plus, from_core_p, stage_p, from_z_p))

        def z_peer(step):
            return lax.rem(z + step, z_count)

        def rows_of(target):
            return pl.ds(pl.multiple_of(target * share, share), share)

        def c_copy(side, step):
            acc, landing, _, _ = sides[side]
            to_z = z_peer(step)
            return pltpu.make_async_remote_copy(
                src_ref=acc.at[:, rows_of(2 * to_z + 1 - core), :],
                dst_ref=landing.at[step],
                send_sem=c_send.at[side, step],
                recv_sem=c_recv.at[side, step],
                device_id=(blk, 2 * z + 1 - core),
                device_id_type=mesh_ids,
            )

        def z_copy(side, step, to_z, slot):
            _, _, stage, landing = sides[side]
            return pltpu.make_async_remote_copy(
                src_ref=stage.at[step],
                dst_ref=landing.at[slot],
                send_sem=z_send.at[side, step],
                recv_sem=z_recv.at[side, slot],
                device_id=(blk, 2 * to_z + core),
                device_id_type=mesh_ids,
            )

        def z_direct(side, step):
            return z_copy(side, step, z_peer(step), step)

        def chip_terms(side, step):
            acc, landing, _, _ = sides[side]
            c_copy(side, step).wait_recv()
            return acc[:, rows_of(2 * z_peer(step) + core), :] + landing[step]

        def fill(side, step, value):
            sides[side][2][step] = value.reshape(-1, value.shape[-1]).astype(bf)

        def add_from(side, total, slot):
            z_direct(side, slot).wait_recv()
            return total + sides[side][3][slot].astype(jnp.float32).reshape(total.shape)

        order = list(range(1, z_count)) + [0]
        relayed = z_count == 4
        inward = jnp.where(z < 2, 1, 3)
        outward = 4 - inward
        is_end = (z == 0) | (z == 3)
        last = chunks - 1

        def minus_done():
            for step in order:
                c_copy(0, step).start()

        work(last, minus_done)
        for step in order:
            c_copy(1, step).start()

        for side in range(2):
            if relayed:
                @pl.when(is_end)
                def _():
                    fill(side, outward, chip_terms(side, outward))
                    z_copy(side, outward, z_peer(inward), 0).start()
                    for step in (2, inward):
                        fill(side, step, chip_terms(side, step))
                        z_direct(side, step).start()

                @pl.when(jnp.logical_not(is_end))
                def _():
                    fill(side, inward, chip_terms(side, inward))
                    z_direct(side, inward).start()
                    far = chip_terms(side, 2)
                    fill(side, 2, add_from(side, far, 0))
                    z_direct(side, 2).start()
                    fill(side, outward, chip_terms(side, outward))
                    z_direct(side, outward).start()
            else:
                for step in order[:-1]:
                    fill(side, step, chip_terms(side, step))
                    z_direct(side, step).start()

        def finish(side, into):
            acc, landing, _, _ = sides[side]
            c_copy(side, 0).wait_recv()
            total = acc[:, rows_of(seg), :] + landing[0]
            if relayed:
                total = add_from(side, total, outward)
                total = add_from(side, total, 2)
                into[...] = total

                @pl.when(jnp.logical_not(is_end))
                def _():
                    into[...] = add_from(side, into[...], inward)
            else:
                for step in range(1, z_count):
                    total = add_from(side, total, step)
                into[...] = total

        def o_copy(step):
            return pltpu.make_async_remote_copy(
                src_ref=done,
                dst_ref=others_ref.at[blk],
                send_sem=o_send.at[step],
                recv_sem=o_recv.at[step],
                device_id=(blk_peer(step), seg),
                device_id_type=mesh_ids,
            )

        keep = pltpu.make_async_copy(done, others_ref.at[blk], own_sem)
        finish(0, done)
        for step in range(1, blk_count):
            o_copy(step).start()
        keep.start()
        keep.wait()
        for step in range(1, blk_count):
            o_copy(step).wait()
        theirs = others_ref[came_from]
        got = lag_order(
            [theirs[c, :, a * chan : (a + 1) * chan] for a in range(COARSE) for c in reversed(range(2 * FINE))]
        ) * scaling
        out_ref[0] = got
        finish(1, done_p)
        total = done_p[...]
        own = lag_order(
            [total[a, :, c * chan : (c + 1) * chan] for a in range(COARSE) for c in range(2 * FINE)]
        ) * scaling
        got = out_ref[0]
        out_ref[0] = jnp.where(parity == 0, own, got)
        out_ref[1] = jnp.where(parity == 0, got, own)
        for side in range(2):
            for step in order:
                c_copy(side, step).wait_send()
            for step in order[:-1]:
                z_direct(side, step).wait_send()
    else:
        work(chunks - 1)
        plus_out[...] = plus[...]
        minus_out[...] = minus[...]
        picks_out[0] = came_from
        picks_out[1] = parity

    pl.loop(chunks - ahead, chunks)(a_sent)

    @pl.loop(0, chunks)
    def _(k):
        for step in range(1, blk_count):
            b_copy(k, step).wait_send()


def correlate(rows, pairing, fibre_lists, bound, tail, scaling):
    held, frequencies = rows.shape[1], rows.shape[3]
    chan = fibre_lists.shape[1]
    blk_count, seg_count = lax.axis_size("blk"), lax.axis_size("seg")
    chunks = frequencies // CHUNK
    cos, sin = phase_tables(frequencies)

    def by_chunk(table):
        return np.ascontiguousarray(table.reshape(-1, chunks, CHUNK).transpose(1, 0, 2))

    slots = np.arange(2 * seg_count * held)
    number = slots // 2
    part = slots % 2
    across = np.broadcast_to(number[:, None], (slots.size, slots.size))
    places = np.concatenate([number[None], part[None], across]).astype(np.int32)

    wide = COARSE * chan
    f32, bf = jnp.float32, jnp.bfloat16
    share = chan // seg_count
    z_count = seg_count // 2
    plus_shape, minus_shape = (COARSE, chan, 2 * wide), (2 * FINE, chan, wide)
    p_shape, m_shape = (COARSE, share, 2 * wide), (2 * FINE, share, wide)
    dma = pltpu.SemaphoreType.DMA
    in_vmem, anywhere = pl.BlockSpec(memory_space=pltpu.VMEM), pl.BlockSpec(memory_space=pl.ANY)
    in_smem, picked = pl.BlockSpec(memory_space=pltpu.SMEM), jax.ShapeDtypeStruct((2,), jnp.int32)
    scratch = [
        pltpu.VMEM((blk_count * 2 * bound, 2 * seg_count * held), bf),
        pltpu.VMEM((4 * chan, blk_count * 2 * bound), bf),
        pltpu.VMEM((chunks, seg_count * held, 2, CHUNK), bf),
        pltpu.VMEM((chunks, blk_count, 2 * bound, CHUNK), bf),
        pltpu.VMEM((chunks, blk_count, 2 * bound, CHUNK), bf),
        pltpu.VMEM((wide, 2 * CHUNK), bf),
        pltpu.VMEM((wide, 2 * CHUNK), bf),
        pltpu.VMEM((2 * wide, 2 * CHUNK), bf),
        pltpu.VMEM(plus_shape, f32),
        pltpu.VMEM(minus_shape, f32),
        dma((chunks, seg_count)),
        dma((chunks, seg_count)),
        dma((chunks, blk_count)),
        dma((chunks, blk_count)),
        dma((chunks,)),
    ]
    if tail:
        out_shape = [jax.ShapeDtypeStruct((2, share, chan, LH), f32)]
        out_specs = [in_vmem]
        flat_p, flat_m = (COARSE * share, 2 * wide), (2 * FINE * share, wide)
        scratch += [
            pltpu.VMEM((z_count,) + m_shape, f32),
            pltpu.VMEM((z_count,) + p_shape, f32),
            pltpu.VMEM((z_count,) + flat_m, bf),
            pltpu.VMEM((z_count,) + flat_p, bf),
            pltpu.VMEM((z_count,) + flat_m, bf),
            pltpu.VMEM((z_count,) + flat_p, bf),
            pltpu.VMEM(m_shape, f32),
            pltpu.VMEM(p_shape, f32),
            pltpu.VMEM((blk_count,) + m_shape, f32),
            dma((2, z_count)),
            dma((2, z_count)),
            dma((2, z_count)),
            dma((2, z_count)),
            dma((blk_count,)),
            dma((blk_count,)),
            dma(()),
        ]
    else:
        out_shape = [jax.ShapeDtypeStruct(plus_shape, f32), jax.ShapeDtypeStruct(minus_shape, f32), picked]
        out_specs = [in_vmem, in_vmem, in_smem]
    return pl.pallas_call(
        functools.partial(fused_kernel, chan, bound, tail, scaling),
        in_specs=[anywhere, in_smem] + [in_vmem] * 4,
        out_specs=out_specs,
        out_shape=out_shape,
        scratch_shapes=scratch,
        compiler_params=pltpu.CompilerParams(
            collective_id=0, has_side_effects=True, vmem_limit_bytes=56 * 1024 * 1024
        ),
        cost_estimate=pl.CostEstimate(
            flops=8 * wide * wide * frequencies * 2, bytes_accessed=16 * wide * wide, transcendentals=0
        ),
    )(rows, pairing, fibre_lists, places, by_chunk(cos), by_chunk(sin))


def local(spectra, fibre_lists, pairing):
    seg_all, frequencies = spectra.shape[0], spectra.shape[3]
    blk_count, seg_count = lax.axis_size("blk"), lax.axis_size("seg")
    chan = fibre_lists.shape[1]
    bound = 2 * (3 * chan // (2 * blk_count))

    share = chan // seg_count
    tail = share % 8 == 0
    scaling = 1.0 / math.sqrt(frequencies * seg_all)
    results = correlate(spectra, pairing, fibre_lists, bound, tail, scaling)
    if tail:
        return results[0][None]
    plus, minus, chosen = results
    plus = lax.psum_scatter(plus, "seg", scatter_dimension=1, tiled=True)
    minus = lax.psum_scatter(minus, "seg", scatter_dimension=1, tiled=True)
    others = lax.all_gather(minus, "blk", axis=0)
    other = lax.dynamic_index_in_dim(others, chosen[0], 0, keepdims=False)
    own = plus.reshape(COARSE, share, 2 * FINE, chan)
    own = jnp.transpose(own, (1, 3, 0, 2)).reshape(share, chan, LH) * scaling
    got = other.reshape(2 * FINE, share, COARSE, chan)[::-1]
    got = jnp.transpose(got, (1, 3, 2, 0)).reshape(share, chan, LH) * scaling
    first = chosen[1] == 0
    return jnp.stack([jnp.where(first, own, got), jnp.where(first, got, own)])[None]


def solution(mesh):
    in_specs = (P(None, ("blk", "seg"), None, None), P(), P())
    out_specs = P(None, "blk", "seg", None, None)
    return jax.shard_map(local, mesh=mesh, in_specs=in_specs, out_specs=out_specs, check_vma=False)
```

```python
import functools
import math

import numpy as np
import jax
import jax.numpy as jnp
from jax import lax
from jax.experimental import pallas as pl
from jax.experimental.pallas import tpu as pltpu
from jax.sharding import PartitionSpec as P

LH = 128
STEP = 16
COARSE = LH // STEP
FINE = STEP // 2
CHUNK = 256
AHEAD = 6
NT = (((1,), (1,)), ((), ()))


def phase_tables(frequencies):
    freq = np.arange(frequencies, dtype=np.float64)[None, :]
    coarse = (STEP * np.arange(COARSE, dtype=np.float64) + (STEP - 1) / 2)[:, None]
    fine = (np.arange(FINE, dtype=np.float64) + 0.5)[:, None]
    angles = np.concatenate([coarse, fine], 0) * freq * (math.pi / frequencies)
    return np.cos(angles).astype(np.float32), np.sin(angles).astype(np.float32)


def plan(chan, bound, width, blk, blk_count, pairing, lists, places, pack, unpack):
    count = lists.shape[0]
    lists_t = jnp.swapaxes(lists[...], 0, 1)
    i32, f32, bf = jnp.int32, jnp.float32, jnp.bfloat16

    def lowest(block):
        least = block
        at = block
        for _ in range(count // 2 - 1):
            at = pairing[0, at] ^ 1
            least = jnp.minimum(least, at)
        return least

    least = [lowest(jnp.int32(b)) for b in range(count)]
    owner = [
        jnp.where(least[b] < least[b ^ 1], jnp.int32(b), pairing[0, b]) // 2 for b in range(count)
    ]
    lead = jnp.int32(0)
    came_from = jnp.int32(0)
    for k in range(blk_count):
        first = least[2 * k] < least[2 * k + 1]
        lead = jnp.where(blk == k, jnp.where(first, 2 * k, 2 * k + 1), lead)
        came_from = jnp.where(blk == k, jnp.where(first, owner[2 * k + 1], owner[2 * k]), came_from)
    follow = pairing[0, lead]

    columns = places.shape[1]
    number = places[0:1, :]
    pair_of = jnp.zeros((1, columns), i32)
    for b in range(count):
        hit = lists_t[:, b : b + 1] == number + blk * width
        pair_of = pair_of + jnp.sum(jnp.where(hit, owner[b], 0), axis=0, keepdims=True)
    kinds = max(8, blk_count)
    real = (lax.broadcasted_iota(i32, (kinds, columns), 0) == pair_of) & (places[1:2, :] == 0)
    before = places[2 : 2 + columns, :] < number
    ranks = jnp.dot(
        jnp.where(real, 1.0, 0.0).astype(bf),
        jnp.where(before, 1.0, 0.0).astype(bf),
        preferred_element_type=f32,
    )
    mine = lax.broadcasted_iota(i32, (kinds, columns), 0) == pair_of
    rank = jnp.sum(jnp.where(mine, ranks, 0.0), axis=0, keepdims=True).astype(i32)
    target = pair_of * (2 * bound) + places[1:2, :] * bound + rank
    pack[...] = jnp.where(lax.broadcasted_iota(i32, pack.shape, 0) == target, 1.0, 0.0).astype(bf)

    roles = (lead, follow)
    zero_col, zero_row = jnp.zeros((chan, 1), i32), jnp.zeros((1, chan), i32)
    tall = [sum((jnp.where(role == b, lists_t[:, b : b + 1], 0) for b in range(count)), zero_col) for role in roles]
    flat = [sum((jnp.where(role == b, lists[b : b + 1, :], 0) for b in range(count)), zero_row) for role in roles]
    shift = width.bit_length() - 1
    lane = lax.broadcasted_iota(i32, (chan, unpack.shape[1]), 1)
    for r in range(2):
        rank = zero_col
        for other in flat:
            ahead = ((tall[r] >> shift) == (other >> shift)) & (other < tall[r])
            rank = rank + jnp.sum(jnp.where(ahead, 1, 0), axis=1, keepdims=True)
        spot = (tall[r] >> shift) * (2 * bound) + rank
        for part in range(2):
            hit = lane == spot + part * bound
            unpack[(2 * part + r) * chan : (2 * part + r + 1) * chan, :] = jnp.where(hit, 1.0, 0.0).astype(bf)
    return came_from, lead & 1


def lag_order(blocks):
    return jnp.swapaxes(jnp.swapaxes(jnp.stack(blocks), 0, 1), 1, 2)


def fused_kernel(
    chan, bound, tail, scaling, rows_ref, pairing, lists, places, cos_ref, sin_ref, *rest
):
    if tail:
        out_ref, *rest = rest
    else:
        plus_out, minus_out, picks_out, *rest = rest
    pack, unpack, col, packed, arr, xp, xm, yp, plus, minus, a_send, a_recv, b_send, b_recv, local_sem, *rest = rest
    blk_count, seg_count = lax.axis_size("blk"), lax.axis_size("seg")
    blk, seg = lax.axis_index("blk"), lax.axis_index("seg")
    chunks = col.shape[0]
    held = rows_ref.shape[1]
    width = col.shape[3]
    bf = jnp.bfloat16
    mesh_ids = pl.DeviceIdType.MESH

    def seg_peer(step):
        return lax.rem(seg + step, seg_count)

    def blk_peer(step):
        return lax.rem(blk + step, blk_count)

    barrier = pltpu.get_barrier_semaphore()
    for step in range(1, seg_count):
        pl.semaphore_signal(barrier, inc=1, device_id=(blk, seg_peer(step)), device_id_type=mesh_ids)
    for step in range(1, blk_count):
        pl.semaphore_signal(barrier, inc=1, device_id=(blk_peer(step), seg), device_id_type=mesh_ids)
    pl.semaphore_wait(barrier, seg_count + blk_count - 2)

    def a_copy(k, step):
        to = seg_peer(step)
        return pltpu.make_async_remote_copy(
            src_ref=rows_ref.at[to, :, :, pl.ds(pl.multiple_of(k * width, width), width)],
            dst_ref=col.at[k, pl.ds(pl.multiple_of(seg * held, held), held)],
            send_sem=a_send.at[k, step],
            recv_sem=a_recv.at[k, step],
            device_id=(blk, to),
            device_id_type=mesh_ids,
        )

    def a_own(k):
        return pltpu.make_async_copy(
            rows_ref.at[seg, :, :, pl.ds(pl.multiple_of(k * width, width), width)],
            col.at[k, pl.ds(pl.multiple_of(seg * held, held), held)],
            local_sem.at[k],
        )

    def b_copy(k, step):
        to = blk_peer(step)
        return pltpu.make_async_remote_copy(
            src_ref=packed.at[k, to],
            dst_ref=arr.at[k, blk],
            send_sem=b_send.at[k, step],
            recv_sem=b_recv.at[k, step],
            device_id=(to, seg),
            device_id_type=mesh_ids,
        )

    def b_own(k):
        return pltpu.make_async_copy(packed.at[k, blk], arr.at[k, blk], b_send.at[k, 0])

    def launch(k):
        for step in range(1, seg_count):
            a_copy(k, step).start()
        a_own(k).start()

    ahead = min(AHEAD, chunks)
    pl.loop(0, ahead)(launch)

    plus[...] = jnp.zeros_like(plus)
    minus[...] = jnp.zeros_like(minus)
    came_from, parity = plan(chan, bound, seg_count * held, blk, blk_count, pairing, lists, places, pack, unpack)

    def route(k):
        for step in range(1, seg_count):
            a_copy(k, step).wait_recv()
        a_own(k).wait()
        mixed = jnp.dot(pack[...], col[k].reshape(2 * seg_count * held, width), preferred_element_type=jnp.float32).astype(bf)
        packed[k] = mixed.reshape(blk_count, 2 * bound, width)
        for step in range(1, blk_count):
            b_copy(k, step).start()
        b_own(k).start()

    def work(k, minus_done=None):
        for step in range(1, blk_count):
            b_copy(k, step).wait_recv()
        b_own(k).wait()
        block = arr[k].reshape(blk_count * 2 * bound, width)
        rows = jnp.dot(unpack[...], block, preferred_element_type=jnp.float32)
        xr, yr = rows[0:chan], rows[chan : 2 * chan]
        xi, yi = rows[2 * chan : 3 * chan], rows[3 * chan : 4 * chan]
        re, im = pl.ds(0, width), pl.ds(width, width)
        for a in range(COARSE):
            c, s = cos_ref[k, a : a + 1, :], sin_ref[k, a : a + 1, :]
            rc, rs, ic, i_s = xr * c, xr * s, xi * c, xi * s
            at = pl.ds(a * chan, chan)
            xp[at, re] = (rc - i_s).astype(bf)
            xp[at, im] = (ic + rs).astype(bf)
            xm[at, re] = (rc + i_s).astype(bf)
            xm[at, im] = (ic - rs).astype(bf)
        for m in range(COARSE, COARSE + FINE):
            c, s = cos_ref[k, m : m + 1, :], sin_ref[k, m : m + 1, :]
            rc, rs, ic, i_s = yr * c, yr * s, yi * c, yi * s
            at, back = pl.ds((FINE + m - COARSE) * chan, chan), pl.ds((FINE - 1 - m + COARSE) * chan, chan)
            yp[at, re] = (rc + i_s).astype(bf)
            yp[at, im] = (ic - rs).astype(bf)
            yp[back, re] = (rc - i_s).astype(bf)
            yp[back, im] = (ic + rs).astype(bf)
        tile = 4 * chan

        @pl.loop(0, xm.shape[0] // tile, unroll=2)
        def _(t):
            at = pl.ds(pl.multiple_of(t * tile, tile), tile)
            term = lax.dot_general(yp[...], xm[at, :], NT, preferred_element_type=jnp.float32)
            minus[:, :, at] += term.reshape(2 * FINE, chan, tile)

        if minus_done:
            minus_done()

        @pl.loop(0, yp.shape[0] // tile, unroll=2)
        def _(t):
            at = pl.ds(pl.multiple_of(t * tile, tile), tile)
            term = lax.dot_general(xp[...], yp[at, :], NT, preferred_element_type=jnp.float32)
            plus[:, :, at] += term.reshape(COARSE, chan, tile)

    def a_sent(k):
        for step in range(1, seg_count):
            a_copy(k, step).wait_send()

    route(0)

    @pl.loop(1, chunks)
    def _(k):
        @pl.when(k + ahead - 1 < chunks)
        def _():
            a_sent(k - 1)
            launch(k + ahead - 1)

        route(k)
        work(k - 1)

    if tail:
        from_core_m, from_core_p, stage_m, stage_p, from_z_m, from_z_p, done, done_p, others_ref, c_send, c_recv, z_send, z_recv, o_send, o_recv, own_sem = rest
        share = chan // seg_count
        z_count = seg_count // 2
        core, z = lax.rem(seg, 2), lax.div(seg, 2)
        sides = ((minus, from_core_m, stage_m, from_z_m), (plus, from_core_p, stage_p, from_z_p))

        def z_peer(step):
            return lax.rem(z + step, z_count)

        def rows_of(target):
            return pl.ds(pl.multiple_of(target * share, share), share)

        def c_copy(side, step):
            acc, landing, _, _ = sides[side]
            to_z = z_peer(step)
            return pltpu.make_async_remote_copy(
                src_ref=acc.at[:, rows_of(2 * to_z + 1 - core), :],
                dst_ref=landing.at[step],
                send_sem=c_send.at[side, step],
                recv_sem=c_recv.at[side, step],
                device_id=(blk, 2 * z + 1 - core),
                device_id_type=mesh_ids,
            )

        def z_copy(side, step, to_z, slot):
            _, _, stage, landing = sides[side]
            return pltpu.make_async_remote_copy(
                src_ref=stage.at[step],
                dst_ref=landing.at[slot],
                send_sem=z_send.at[side, step],
                recv_sem=z_recv.at[side, slot],
                device_id=(blk, 2 * to_z + core),
                device_id_type=mesh_ids,
            )

        def z_direct(side, step):
            return z_copy(side, step, z_peer(step), step)

        def chip_terms(side, step):
            acc, landing, _, _ = sides[side]
            c_copy(side, step).wait_recv()
            return acc[:, rows_of(2 * z_peer(step) + core), :] + landing[step]

        def fill(side, step, value):
            sides[side][2][step] = value.reshape(-1, value.shape[-1]).astype(bf)

        def add_from(side, total, slot):
            z_direct(side, slot).wait_recv()
            return total + sides[side][3][slot].astype(jnp.float32).reshape(total.shape)

        order = list(range(1, z_count)) + [0]
        relayed = z_count == 4
        inward = jnp.where(z < 2, 1, 3)
        outward = 4 - inward
        is_end = (z == 0) | (z == 3)
        last = chunks - 1

        def minus_done():
            for step in order:
                c_copy(0, step).start()

        work(last, minus_done)
        for step in order:
            c_copy(1, step).start()

        for side in range(2):
            if relayed:
                @pl.when(is_end)
                def _():
                    fill(side, outward, chip_terms(side, outward))
                    z_copy(side, outward, z_peer(inward), 0).start()
                    for step in (2, inward):
                        fill(side, step, chip_terms(side, step))
                        z_direct(side, step).start()

                @pl.when(jnp.logical_not(is_end))
                def _():
                    fill(side, inward, chip_terms(side, inward))
                    z_direct(side, inward).start()
                    far = chip_terms(side, 2)
                    fill(side, 2, add_from(side, far, 0))
                    z_direct(side, 2).start()
                    fill(side, outward, chip_terms(side, outward))
                    z_direct(side, outward).start()
            else:
                for step in order[:-1]:
                    fill(side, step, chip_terms(side, step))
                    z_direct(side, step).start()

        def finish(side, into):
            acc, landing, _, _ = sides[side]
            c_copy(side, 0).wait_recv()
            total = acc[:, rows_of(seg), :] + landing[0]
            if relayed:
                total = add_from(side, total, outward)
                total = add_from(side, total, 2)
                into[...] = total

                @pl.when(jnp.logical_not(is_end))
                def _():
                    into[...] = add_from(side, into[...], inward)
            else:
                for step in range(1, z_count):
                    total = add_from(side, total, step)
                into[...] = total

        def o_copy(step):
            return pltpu.make_async_remote_copy(
                src_ref=done,
                dst_ref=others_ref.at[blk],
                send_sem=o_send.at[step],
                recv_sem=o_recv.at[step],
                device_id=(blk_peer(step), seg),
                device_id_type=mesh_ids,
            )

        keep = pltpu.make_async_copy(done, others_ref.at[blk], own_sem)
        finish(0, done)
        for step in range(1, blk_count):
            o_copy(step).start()
        keep.start()
        keep.wait()
        for step in range(1, blk_count):
            o_copy(step).wait()
        theirs = others_ref[came_from]
        got = lag_order(
            [theirs[c, :, a * chan : (a + 1) * chan] for a in range(COARSE) for c in reversed(range(2 * FINE))]
        ) * scaling
        out_ref[0] = got
        finish(1, done_p)
        total = done_p[...]
        own = lag_order(
            [total[a, :, c * chan : (c + 1) * chan] for a in range(COARSE) for c in range(2 * FINE)]
        ) * scaling
        got = out_ref[0]
        out_ref[0] = jnp.where(parity == 0, own, got)
        out_ref[1] = jnp.where(parity == 0, got, own)
        for side in range(2):
            for step in order:
                c_copy(side, step).wait_send()
            for step in order[:-1]:
                z_direct(side, step).wait_send()
    else:
        work(chunks - 1)
        plus_out[...] = plus[...]
        minus_out[...] = minus[...]
        picks_out[0] = came_from
        picks_out[1] = parity

    pl.loop(chunks - ahead, chunks)(a_sent)

    @pl.loop(0, chunks)
    def _(k):
        for step in range(1, blk_count):
            b_copy(k, step).wait_send()


def correlate(rows, pairing, fibre_lists, bound, tail, scaling):
    held, frequencies = rows.shape[1], rows.shape[3]
    chan = fibre_lists.shape[1]
    blk_count, seg_count = lax.axis_size("blk"), lax.axis_size("seg")
    chunks = frequencies // CHUNK
    cos, sin = phase_tables(frequencies)

    def by_chunk(table):
        return np.ascontiguousarray(table.reshape(-1, chunks, CHUNK).transpose(1, 0, 2))

    slots = np.arange(2 * seg_count * held)
    number = slots // 2
    part = slots % 2
    across = np.broadcast_to(number[:, None], (slots.size, slots.size))
    places = np.concatenate([number[None], part[None], across]).astype(np.int32)

    wide = COARSE * chan
    f32, bf = jnp.float32, jnp.bfloat16
    share = chan // seg_count
    z_count = seg_count // 2
    plus_shape, minus_shape = (COARSE, chan, 2 * wide), (2 * FINE, chan, wide)
    p_shape, m_shape = (COARSE, share, 2 * wide), (2 * FINE, share, wide)
    dma = pltpu.SemaphoreType.DMA
    in_vmem, anywhere = pl.BlockSpec(memory_space=pltpu.VMEM), pl.BlockSpec(memory_space=pl.ANY)
    in_smem, picked = pl.BlockSpec(memory_space=pltpu.SMEM), jax.ShapeDtypeStruct((2,), jnp.int32)
    scratch = [
        pltpu.VMEM((blk_count * 2 * bound, 2 * seg_count * held), bf),
        pltpu.VMEM((4 * chan, blk_count * 2 * bound), bf),
        pltpu.VMEM((chunks, seg_count * held, 2, CHUNK), bf),
        pltpu.VMEM((chunks, blk_count, 2 * bound, CHUNK), bf),
        pltpu.VMEM((chunks, blk_count, 2 * bound, CHUNK), bf),
        pltpu.VMEM((wide, 2 * CHUNK), bf),
        pltpu.VMEM((wide, 2 * CHUNK), bf),
        pltpu.VMEM((2 * wide, 2 * CHUNK), bf),
        pltpu.VMEM(plus_shape, f32),
        pltpu.VMEM(minus_shape, f32),
        dma((chunks, seg_count)),
        dma((chunks, seg_count)),
        dma((chunks, blk_count)),
        dma((chunks, blk_count)),
        dma((chunks,)),
    ]
    if tail:
        out_shape = [jax.ShapeDtypeStruct((2, share, chan, LH), f32)]
        out_specs = [in_vmem]
        flat_p, flat_m = (COARSE * share, 2 * wide), (2 * FINE * share, wide)
        scratch += [
            pltpu.VMEM((z_count,) + m_shape, f32),
            pltpu.VMEM((z_count,) + p_shape, f32),
            pltpu.VMEM((z_count,) + flat_m, bf),
            pltpu.VMEM((z_count,) + flat_p, bf),
            pltpu.VMEM((z_count,) + flat_m, bf),
            pltpu.VMEM((z_count,) + flat_p, bf),
            pltpu.VMEM(m_shape, f32),
            pltpu.VMEM(p_shape, f32),
            pltpu.VMEM((blk_count,) + m_shape, f32),
            dma((2, z_count)),
            dma((2, z_count)),
            dma((2, z_count)),
            dma((2, z_count)),
            dma((blk_count,)),
            dma((blk_count,)),
            dma(()),
        ]
    else:
        out_shape = [jax.ShapeDtypeStruct(plus_shape, f32), jax.ShapeDtypeStruct(minus_shape, f32), picked]
        out_specs = [in_vmem, in_vmem, in_smem]
    return pl.pallas_call(
        functools.partial(fused_kernel, chan, bound, tail, scaling),
        in_specs=[anywhere, in_smem] + [in_vmem] * 4,
        out_specs=out_specs,
        out_shape=out_shape,
        scratch_shapes=scratch,
        compiler_params=pltpu.CompilerParams(
            collective_id=0, has_side_effects=True, vmem_limit_bytes=56 * 1024 * 1024
        ),
        cost_estimate=pl.CostEstimate(
            flops=8 * wide * wide * frequencies * 2, bytes_accessed=16 * wide * wide, transcendentals=0
        ),
    )(rows, pairing, fibre_lists, places, by_chunk(cos), by_chunk(sin))


def local(spectra, fibre_lists, pairing):
    seg_all, frequencies = spectra.shape[0], spectra.shape[3]
    blk_count, seg_count = lax.axis_size("blk"), lax.axis_size("seg")
    chan = fibre_lists.shape[1]
    bound = 2 * (3 * chan // (2 * blk_count))

    share = chan // seg_count
    tail = share % 8 == 0
    scaling = 1.0 / math.sqrt(frequencies * seg_all)
    results = correlate(spectra, pairing, fibre_lists, bound, tail, scaling)
    if tail:
        return results[0][None]
    plus, minus, chosen = results
    plus = lax.psum_scatter(plus, "seg", scatter_dimension=1, tiled=True)
    minus = lax.psum_scatter(minus, "seg", scatter_dimension=1, tiled=True)
    others = lax.all_gather(minus, "blk", axis=0)
    other = lax.dynamic_index_in_dim(others, chosen[0], 0, keepdims=False)
    own = plus.reshape(COARSE, share, 2 * FINE, chan)
    own = jnp.transpose(own, (1, 3, 0, 2)).reshape(share, chan, LH) * scaling
    got = other.reshape(2 * FINE, share, COARSE, chan)[::-1]
    got = jnp.transpose(got, (1, 3, 2, 0)).reshape(share, chan, LH) * scaling
    first = chosen[1] == 0
    return jnp.stack([jnp.where(first, own, got), jnp.where(first, got, own)])[None]


def solution(mesh):
    in_specs = (P(None, ("blk", "seg"), None, None), P(), P())
    out_specs = P(None, "blk", "seg", None, None)
    return jax.shard_map(local, mesh=mesh, in_specs=in_specs, out_specs=out_specs, check_vma=False)
```
